32 devices in a mesh: tile: 8 (over y, x, core), kern: 4 (over z).
Axes of the slice: x: 2, y: 2, z: 4, core: 2. Of those that a mesh axis runs over, the one named last changes fastest.
Arguments:
- mask_field: bfloat16 [512, 2048], P('tile'), may hold values from 0 to 1
- target_map: int32 [512, 2048], P('tile'), may hold values 0 or 1
- kernel_real: bfloat16 [4, 65, 65], P('kern'), may hold values from -0.09375 to 0.09375
- kernel_imag: bfloat16 [4, 65, 65], P('kern'), may hold values from -0.09375 to 0.09375
- socs_weight: float32 [4], replicated, may hold values from 0.05 to 1
- edge_pixel: int32 [32768], P(('tile', 'kern')), may hold values from 0 to 32767
- edge_owner: int32 [32768, 1], P(('tile', 'kern')), may hold values from 0 to 7; in each aligned block of 1024 rows (0 to 1023, 1024 to 2047, ...) at most 256 rows name the same one
- edge_slot: int32 [32768], P(('tile', 'kern')), may hold values from 0 to 255
- edge_weight: float32 [32768], P(('tile', 'kern')), may hold values from -1 to 1
Outputs:
- mask_grad: float32 [512, 2048], P('tile', 'kern')
- polygon_grad: float32 [2048], P('tile')
The draws below stay inside these ranges and needn't reach their ends.
Inputs may be any that keep to these rules, and one draw needn't show every extreme that they name: `edge_owner`: at most 256 edge pixels of one device name the same owner band. `edge_pixel`: Row-major index within the device's own block of mask_grad.
All inputs are finite; a program needn't handle non-finite values. No bound on the sum of `target_map` on one device may be relied on, other than what follows from the above.
Results may differ from the reference program's by a relative error of at most 0.0028.
Values may be sent and summed in bfloat16 or wider, within the bound.
No kernel may reach another device: no remote copies, remote signals or barrier semaphores. Data moves between devices by JAX's collectives and lax.ppermute only.
A program may use at most 64 MiB of HBM per device.

```python
import math
import jax
import jax.numpy as jnp
import numpy as np
from jax import lax

W = 2048
ROWS = 64
RADIUS = 32
KSIZE = 65
KERN_DEV = 1
KERNELS = 4
EDGES_DEV = 1024
POLY_DEV = 256
NY = 512
EDGES = 32768
POLYS = 2048
CAP = 256
N_TILE = 8
N_KERN = 4


def set_ends(values, own_key, low, largest):
    spot = [jax.random.randint(jax.random.fold_in(own_key, axis), (), 0, length) for axis, length in enumerate(values.shape)]
    longest = values.shape.index(max(values.shape))
    neighbour = spot[:longest] + [(spot[longest] + 1) % values.shape[longest]] + spot[longest + 1:]
    return values.at[tuple(spot)].set(low).at[tuple(neighbour)].set(largest)


def level_of(stream_key, extent, shards, least, top_value):
    def one(dim, blocks):
        steps = jax.random.uniform(jax.random.fold_in(jax.random.fold_in(stream_key, 6), dim), (blocks,), jnp.float32, least / len(shards), top_value / len(shards))
        return jnp.repeat(jnp.exp(steps), extent[dim] // blocks).reshape((-1,) + (1,) * (len(extent) - dim - 1))

    loudness = one(*shards[0])
    for cut in shards[1:]:
        loudness = loudness * one(*cut)
    return loudness


def deal_out(own_key, own, number, rows, count, top, reach, skew):
    ranking = jax.random.permutation(own_key, count)
    crowded, common = portions_of(count, rows * top, reach, skew, True), portions_of(count, rows * top, reach, skew, False)
    places = jnp.arange(count)

    def named(lengths, offset_by):
        used = int((lengths > 0).sum())
        fixed = max(1, used // 4)
        moved = fixed + (places - fixed + offset_by * (used - fixed)) % max(1, count - fixed)
        return jnp.zeros((count,), jnp.int32).at[ranking[jnp.where(places < fixed, places, moved)]].set(jnp.asarray(lengths, jnp.int32))

    lengths = jnp.where(number % 4 == 0, named(crowded, number // 4), named(common, number - number // 4 - 1))
    mixed = jax.random.permutation(jax.random.fold_in(own, 3), count)
    source_of, receiver = mixed[0:count // 2 * 2:2], mixed[1:count // 2 * 2:2]
    slack = jnp.minimum(lengths[source_of] - 1, reach - lengths[receiver]) // 2
    slack = jnp.where((source_of == ranking[0]) | (receiver == ranking[0]) | (lengths[receiver] == 0), 0, jnp.maximum(slack, 0))
    moved = jax.random.randint(jax.random.fold_in(own, 4), (count // 2,), 0, 1 << 20) % (slack + 1)
    lengths = lengths.at[source_of].add(-moved).at[receiver].add(moved)
    items = jnp.searchsorted(jnp.cumsum(lengths), jnp.arange(rows * top), side="right").astype(jnp.int32)
    listing = items.reshape(top, rows).T
    listing = listing[jax.random.permutation(jax.random.fold_in(own, 1), rows)]
    offset_by = jax.random.randint(jax.random.fold_in(own, 2), (rows, 1), 0, top)
    return jnp.take_along_axis(listing, (jnp.arange(top)[None, :] + offset_by) % top, axis=1)


def portions_of(amount, total, limit, skew, full):
    weights = [(1 << 20) // math.isqrt(standing ** skew) + 1 for standing in range(1, amount + 1)]
    largest = limit if full else min(limit, max(-(-total // amount), total * weights[0] // sum(weights)))
    least = 1 if total - largest >= amount - 1 else 0
    given, rest = [largest] + [least] * (amount - 1), total - largest - least * (amount - 1)
    while rest > 0:
        free = [i for i in range(1, amount) if given[i] < largest] or [i for i in range(1, amount) if given[i] < limit]
        whole, budget = sum([weights[i] for i in free]), rest
        for i in free:
            addition = min(limit - given[i], max(1, budget * weights[i] // whole), rest)
            given[i] = given[i] + addition
            rest = rest - addition
    return np.array(given)


def centred(rng, extent, deviation, bound, shards=(), kind=jnp.bfloat16):
    factor_of = level_of(rng, extent, shards, -0.22, 0.18) if shards else 1.0
    values = jax.random.normal(rng, extent, jnp.float32) * deviation * factor_of
    return jnp.minimum(jnp.maximum(values, -bound), bound).astype(kind)


def setup_inputs(seed: int = 0) -> dict:
    key_list = jax.random.split(jax.random.key(seed), 10)
    mask_field = jnp.clip(1.0 * jax.random.uniform(key_list[0], (NY, W), jnp.float32) ** level_of(key_list[0], (NY, W), ((0, 8),), -0.2, 0.2), 0.0, 1.0).astype(jnp.bfloat16)
    target_map = set_ends((jax.random.randint(key_list[1], (NY, W), 0, 2) < 1).astype(jnp.int32), jax.random.fold_in(key_list[1], 1), 0, 1)
    kernel_real = centred(key_list[2], (KERNELS, KSIZE, KSIZE), (KSIZE * KSIZE) ** -0.5, 0.09375, ((0, 4),))
    kernel_imag = centred(key_list[3], (KERNELS, KSIZE, KSIZE), (KSIZE * KSIZE) ** -0.5, 0.09375, ((0, 4),))
    socs_weight = jnp.clip(jnp.exp(jax.random.uniform(key_list[4], (KERNELS,), jnp.float32, math.log(0.05), math.log(1.0))), 0.05, 1.0)
    edge_pixel = set_ends(jax.random.randint(key_list[5], (EDGES,), 0, ROWS * (W // N_KERN)), jax.random.fold_in(key_list[5], 1), 0, (ROWS * (W // N_KERN)) - 1).astype(jnp.int32)
    edge_owner_keys = jax.random.split(jax.random.fold_in(key_list[6], 1), EDGES // EDGES_DEV)
    edge_owner_turns = jax.random.permutation(jax.random.fold_in(key_list[6], 3), EDGES // EDGES_DEV)
    edge_owner = jax.vmap(lambda own, number: deal_out(jax.random.fold_in(key_list[6], 2), own, number, EDGES_DEV, N_TILE, 1, CAP, 2))(edge_owner_keys, edge_owner_turns).reshape((EDGES, 1))
    edge_slot = set_ends(jax.random.randint(key_list[7], (EDGES,), 0, POLY_DEV), jax.random.fold_in(key_list[7], 1), 0, POLY_DEV - 1).astype(jnp.int32)
    edge_weight = jnp.clip(jax.random.uniform(key_list[8], (EDGES,), jnp.float32, -1.0, 1.0) * level_of(key_list[8], (EDGES,), ((0, 32),), -0.4, 0.0), -1.0, 1.0)
    return {"mask_field": mask_field, "target_map": target_map, "kernel_real": kernel_real, "kernel_imag": kernel_imag, "socs_weight": socs_weight, "edge_pixel": edge_pixel, "edge_owner": edge_owner, "edge_slot": edge_slot, "edge_weight": edge_weight}


steepness = 8.0
threshold = 0.67


def correlate(source, filters):
    return lax.conv_general_dilated(source[None], filters, (1, 1), ((RADIUS, RADIUS), (RADIUS, RADIUS)), dimension_numbers=("NCHW", "OIHW", "NCHW"), precision=lax.Precision.HIGHEST)[0]


def reference(mask_field, target_map, kernel_real, kernel_imag, socs_weight, edge_pixel, edge_owner, edge_slot, edge_weight):
    mask_float = mask_field.astype(jnp.float32)
    real_groups = kernel_real.reshape(N_KERN, KERN_DEV, KSIZE, KSIZE)
    imag_groups = kernel_imag.reshape(N_KERN, KERN_DEV, KSIZE, KSIZE)
    weight_groups = socs_weight.reshape(N_KERN, KERN_DEV)

    def group_fields(real_taps, imag_taps):
        filters = jnp.concatenate([real_taps, imag_taps], 0).astype(jnp.float32)[:, None]
        return correlate(mask_float[None], filters)

    def forward(running, kernel_group):
        real_taps, imag_taps, weights = kernel_group
        fields = group_fields(real_taps, imag_taps)
        pair_weight = jnp.concatenate([weights, weights])
        return running + jnp.sum(pair_weight[:, None, None] * fields * fields, 0), None

    intensity, _ = lax.scan(forward, jnp.zeros((NY, W), jnp.float32), (real_groups, imag_groups, weight_groups))
    total_weight = jnp.sum(socs_weight)
    resist = jax.nn.sigmoid(steepness * (intensity / total_weight - threshold))
    slope = 2.0 * (resist - target_map.astype(jnp.float32)) * steepness * resist * (1.0 - resist) / total_weight

    def backward(running, kernel_group):
        real_taps, imag_taps, weights = kernel_group
        fields = group_fields(real_taps, imag_taps)
        pair_weight = jnp.concatenate([weights, weights])
        products = ((2.0 * pair_weight)[:, None, None] * slope[None] * fields).astype(jnp.bfloat16)
        flipped = jnp.concatenate([real_taps, imag_taps], 0).astype(jnp.float32)[None, :, ::-1, ::-1]
        return running + correlate(products.astype(jnp.float32), flipped)[0], None

    mask_grad, _ = lax.scan(backward, jnp.zeros((NY, W), jnp.float32), (real_groups, imag_groups, weight_groups))
    block_width = W // N_KERN
    device_of = jnp.arange(EDGES, dtype=jnp.int32) // EDGES_DEV
    pixel_row = (device_of // N_KERN) * ROWS + edge_pixel // block_width
    pixel_col = (device_of % N_KERN) * block_width + edge_pixel % block_width
    edge_value = edge_weight * mask_grad[pixel_row, pixel_col]
    polygon_ids = edge_owner[:, 0] * POLY_DEV + edge_slot
    polygon_grad = jax.ops.segment_sum(edge_value, polygon_ids, num_segments=POLYS)
    return mask_grad, polygon_grad
```

```python
import functools

import jax
import jax.numpy as jnp
from jax import lax
from jax.experimental import pallas as pl
from jax.experimental.pallas import tpu as pltpu
from jax.sharding import PartitionSpec as P

POLY_DEV = 256

steepness = 8.0
threshold = 0.67

F32 = jnp.float32
BF16 = jnp.bfloat16
LANES = 128
SIDE = 128
VMEM = pl.BlockSpec(memory_space=pltpu.VMEM)
SMEM = pl.BlockSpec(memory_space=pltpu.SMEM)


def pack_kernel(block, pos_ref, mask_ref, target_ref, real_ref, imag_ref, out_ref, rest_ref, taps_ref, square):
    rows, width = mask_ref.shape
    half = rows // 2
    first = pos_ref[0] * block
    left = jnp.maximum(first - SIDE, 0)
    right = jnp.minimum(first + block, width - SIDE)
    has_left = first > 0
    has_right = first + block < width
    pieces = (
        (pl.ds(pl.multiple_of(left, LANES), SIDE), slice(0, SIDE), has_left),
        (pl.ds(pl.multiple_of(first, LANES), block), slice(SIDE, SIDE + block), None),
        (pl.ds(pl.multiple_of(right, LANES), SIDE), slice(SIDE + block, 2 * SIDE + block), has_right),
    )
    for source, place, inside in pieces:
        mask = mask_ref[:, source]
        if inside is not None:
            mask = jnp.where(inside, mask.astype(F32), 0.0).astype(BF16)
        out_ref[0:rows, place] = mask
        target = target_ref[:, source].astype(F32).astype(BF16)
        out_ref[rows : rows + half, place] = target[:half]
        rest_ref[:, place] = target[half:]
    ksize = real_ref.shape[1]
    count = real_ref.shape[0]
    for kernel in range(count):
        for part, ref in enumerate((real_ref, imag_ref)):
            square[...] = jnp.zeros_like(square)
            square[0:ksize, 0:ksize] = ref[kernel].astype(F32)
            taps_ref[2 * kernel + part] = square[...].T[: taps_ref.shape[1]].astype(BF16)


def field_kernel(
    block, width, ksize, n_sets, pos_ref, weight_ref, own_ref, next_ref, rest_ref, *refs
):
    tap_refs = refs[:n_sets]
    here_ref, there_ref = refs[n_sets : n_sets + 2]
    taps32, mask_t, target_t, band, fields, products, total = refs[n_sets + 2 :]
    radius = (ksize - 1) // 2
    per_set = tap_refs[0].shape[0]
    pairs = n_sets * per_set // 2
    rows = here_ref.shape[0]
    half = rows // 2
    window = 2 * rows
    span = block + 2 * radius
    chunks = (ksize - 1) // 8
    kern_at = pos_ref[0]
    last = pos_ref[1]

    for index, ref in enumerate(tap_refs):
        taps32[index * per_set : (index + 1) * per_set] = ref[...].astype(F32)
    for piece in range((block + 2 * SIDE) // LANES):
        lanes = slice(piece * LANES, (piece + 1) * LANES)
        both = jnp.concatenate([own_ref[0:rows, lanes], next_ref[0:rows, lanes]], 0)
        mask_t[lanes, :] = both.astype(F32).T
        one = jnp.concatenate([rest_ref[:, lanes], next_ref[rows : rows + half, lanes]], 0)
        target_t[lanes, :] = jnp.concatenate([one, one], 0).astype(F32).T

    out_row = lax.broadcasted_iota(jnp.int32, (rows, window), 0) < half
    in_row = lax.broadcasted_iota(jnp.int32, (rows, window), 1) < rows
    keep = jnp.logical_or(out_row == in_row, last == 0)
    keep = keep.astype(F32)

    def toeplitz(component, column_rows, j):
        row = jnp.broadcast_to(column_rows[j : j + 1], (rows, window))
        return (pltpu.roll(row, 0, 1, stride=1, stride_axis=0) * keep).astype(BF16)

    def build(chunk, carry):
        start = pl.multiple_of(chunk * 8, 8)
        for component in range(2 * pairs):
            column_rows = taps32[component, pl.ds(start, 8), :]
            for j in range(8):
                band[chunk, component * rows : (component + 1) * rows, j * window : (j + 1) * window] = (
                    toeplitz(component, column_rows, j)
                )
        return carry

    lax.fori_loop(0, chunks, build, 0)
    for component in range(2 * pairs):
        column_rows = taps32[component, chunks * 8 : chunks * 8 + 8, :]
        band[chunks, component * rows : (component + 1) * rows, 0:window] = toeplitz(component, column_rows, 0)

    nt = (((1,), (1,)), ((), ()))
    base = SIDE - 2 * radius
    tail = mask_t[base + chunks * 8 : base + chunks * 8 + span, :].astype(BF16)
    fields[...] = lax.dot_general(tail, band[chunks, :, 0:window], nt, preferred_element_type=F32)

    def forward(chunk, carry):
        start = pl.multiple_of(base + chunk * 8, 8)
        parts = [mask_t[pl.ds(start + j, span), :].astype(BF16) for j in range(8)]
        left = jnp.concatenate(parts, 1)
        fields[...] += lax.dot_general(left, band[chunk], nt, preferred_element_type=F32)
        return carry

    lax.fori_loop(0, chunks, forward, 0)

    weights = []
    for index in range(n_sets):
        source = lax.rem(kern_at - index + n_sets, n_sets)
        for kernel in range(per_set // 2):
            weights.append(weight_ref[source * (per_set // 2) + kernel])
    total_weight = weight_ref[0]
    for kernel in range(1, pairs):
        total_weight = total_weight + weight_ref[kernel]
    total_weight = jnp.full((1, window), total_weight, F32)
    intensity = jnp.zeros((span, window), F32)
    for kernel in range(pairs):
        field = fields[:, kernel * window : (kernel + 1) * window]
        intensity = intensity + weights[kernel] * field * field
    intensity = intensity + pltpu.roll(intensity, rows, 1)
    resist = jax.nn.sigmoid(steepness * (intensity / total_weight - threshold))
    target = target_t[SIDE - radius : SIDE - radius + span, :]
    slope = 2.0 * (resist - target) * steepness * resist * (1.0 - resist) / total_weight
    column = kern_at * block - radius + lax.broadcasted_iota(jnp.int32, (span, window), 0)
    slope = jnp.where(jnp.logical_and(column >= 0, column < width), slope, 0.0)
    for kernel in range(pairs):
        lanes = slice(kernel * window, (kernel + 1) * window)
        products[:, lanes] = ((2.0 * weights[kernel]) * slope * fields[:, lanes]).astype(BF16)

    total[...] = jnp.zeros_like(total)
    total[chunks * 8 : chunks * 8 + span, :] = jnp.dot(
        products[...], band[chunks, :, 0:window], preferred_element_type=F32
    )

    def adjoint(chunk, carry):
        start = pl.multiple_of(chunk * 8, 8)
        for j in range(0, 8, 2):
            two = jnp.dot(
                products[...], band[chunk, :, j * window : (j + 2) * window], preferred_element_type=F32
            )
            total[pl.ds(start + j, span), :] += two[:, :window]
            total[pl.ds(start + j + 1, span), :] += two[:, window:]
        return carry

    lax.fori_loop(0, chunks, adjoint, 0)
    for piece in range(block // LANES):
        lanes = slice(piece * LANES, (piece + 1) * LANES)
        turned = total[2 * radius + piece * LANES : 2 * radius + (piece + 1) * LANES, :].T
        here_ref[:, lanes] = turned[:rows]
        there_ref[:, lanes] = turned[rows:]


def split3(value):
    high = value.astype(BF16)
    rest = value - high.astype(F32)
    middle = rest.astype(BF16)
    low = (rest - middle.astype(F32)).astype(BF16)
    return high, middle, low


def edge_kernel(here_ref, came_ref, pixel_ref, owner_ref, slot_ref, weight_ref, grad_ref, sums_ref):
    rows, block = grad_ref.shape
    tiles, slots = sums_ref.shape
    grad = here_ref[...] + came_ref[...]
    grad_ref[...] = grad
    edges = pixel_ref.shape[1]
    pixel = pixel_ref[...]
    row = pixel // block
    col = pixel - row * block
    row_hit = (lax.broadcasted_iota(jnp.int32, (rows, edges), 0) == row).astype(F32).astype(BF16)
    col_hit = lax.broadcasted_iota(jnp.int32, (block, edges), 0) == col
    tn = (((0,), (0,)), ((), ()))
    picked = jnp.zeros((block, edges), F32)
    for part in split3(grad):
        picked = picked + lax.dot_general(part, row_hit, tn, preferred_element_type=F32)
    value = jnp.sum(jnp.where(col_hit, picked, 0.0), 0, keepdims=True) * weight_ref[...]
    owner_hit = lax.broadcasted_iota(jnp.int32, (tiles, edges), 0) == owner_ref[...]
    slot_hit = (lax.broadcasted_iota(jnp.int32, (slots, edges), 0) == slot_ref[...]).astype(F32).astype(BF16)
    nt = (((1,), (1,)), ((), ()))
    spread = jnp.where(owner_hit, value, 0.0)
    sums = jnp.zeros((tiles, slots), F32)
    for part in split3(spread):
        sums = sums + lax.dot_general(part, slot_hit, nt, preferred_element_type=F32)
    sums_ref[...] = sums


def on_device(
    mask_field,
    target_map,
    kernel_real,
    kernel_imag,
    socs_weight,
    edge_pixel,
    edge_owner,
    edge_slot,
    edge_weight,
):
    rows, width = mask_field.shape
    count, ksize = kernel_real.shape[:2]
    tiles, kerns = lax.axis_size("tile"), lax.axis_size("kern")
    block = width // kerns
    radius = (ksize - 1) // 2
    span = block + 2 * radius
    whole = block + 2 * SIDE
    kern_at = lax.axis_index("kern")
    tile_at = lax.axis_index("tile")
    place = jnp.stack([kern_at, (tile_at == tiles - 1).astype(jnp.int32)]).astype(jnp.int32)
    tap_rows = -(-ksize // 8) * 8
    own, rest, taps = pl.pallas_call(
        functools.partial(pack_kernel, block),
        out_shape=(
            jax.ShapeDtypeStruct((rows + rows // 2, whole), BF16),
            jax.ShapeDtypeStruct((rows // 2, whole), BF16),
            jax.ShapeDtypeStruct((2 * count, tap_rows, LANES), BF16),
        ),
        in_specs=[SMEM] + [VMEM] * 4,
        out_specs=(VMEM,) * 3,
        scratch_shapes=[pltpu.VMEM((LANES, LANES), F32)],
        name="pack",
    )(place, mask_field, target_map, kernel_real, kernel_imag)

    following = lax.ppermute(own, "tile", [(i, (i - 1) % tiles) for i in range(tiles)])
    tap_sets = [taps] + [
        lax.ppermute(taps, "kern", [(i, (i + step) % kerns) for i in range(kerns)])
        for step in range(1, kerns)
    ]
    components = 2 * count * kerns
    chunks = (ksize - 1) // 8
    band_bytes = (chunks + 1) * components * rows * 8 * LANES * 2
    here, there = pl.pallas_call(
        functools.partial(field_kernel, block, width, ksize, kerns),
        out_shape=(jax.ShapeDtypeStruct((rows, block), F32),) * 2,
        in_specs=[SMEM, SMEM] + [VMEM] * (3 + kerns),
        out_specs=(VMEM,) * 2,
        scratch_shapes=[
            pltpu.VMEM((components, tap_rows, LANES), F32),
            pltpu.VMEM((whole, LANES), F32),
            pltpu.VMEM((whole, LANES), F32),
            pltpu.VMEM((chunks + 1, components * rows, 8 * LANES), BF16),
            pltpu.VMEM((span, components * rows), F32),
            pltpu.VMEM((span, components * rows), BF16),
            pltpu.VMEM((span + 2 * radius, LANES), F32),
        ],
        compiler_params=pltpu.CompilerParams(vmem_limit_bytes=band_bytes + (20 << 20)),
        name="fields",
    )(place, socs_weight, own, following, rest, *tap_sets)
    came = lax.ppermute(there, "tile", [(i, (i + 1) % tiles) for i in range(tiles)])
    mask_grad, sums = pl.pallas_call(
        edge_kernel,
        out_shape=(
            jax.ShapeDtypeStruct((rows, block), F32),
            jax.ShapeDtypeStruct((tiles, POLY_DEV), F32),
        ),
        in_specs=[VMEM] * 6,
        out_specs=(VMEM,) * 2,
        name="edges",
    )(
        here,
        came,
        edge_pixel[None, :],
        edge_owner.reshape(1, -1),
        edge_slot[None, :],
        edge_weight[None, :],
    )
    spread = jnp.repeat(sums, kerns, axis=0)
    got = lax.all_to_all(spread, ("tile", "kern"), 0, 0, tiled=True)
    return (mask_grad, jnp.sum(got, 0))


def solution(mesh):
    placed = (
        P("tile", None),
        P("tile", None),
        P("kern", None, None),
        P("kern", None, None),
        P(),
        P(("tile", "kern")),
        P(("tile", "kern"), None),
        P(("tile", "kern")),
        P(("tile", "kern")),
    )
    return jax.shard_map(
        on_device,
        mesh=mesh,
        in_specs=placed,
        out_specs=(P("tile", "kern"), P("tile")),
        check_vma=False,
    )
```

```python
import functools

import jax
import jax.numpy as jnp
from jax import lax
from jax.experimental import pallas as pl
from jax.experimental.pallas import tpu as pltpu
from jax.sharding import PartitionSpec as P

POLY_DEV = 256

steepness = 8.0
threshold = 0.67

F32 = jnp.float32
BF16 = jnp.bfloat16
LANES = 128
SIDE = 64
GROUP = 16
FACTS = 7
ANY = pl.BlockSpec(memory_space=pl.ANY)
VMEM = pl.BlockSpec(memory_space=pltpu.VMEM)
SMEM = pl.BlockSpec(memory_space=pltpu.SMEM)


def split3(value):
    high = value.astype(BF16)
    rest = value - high.astype(F32)
    middle = rest.astype(BF16)
    low = (rest - middle.astype(F32)).astype(BF16)
    return high, middle, low


def split2(value):
    high = value.astype(BF16)
    return high, (value - high.astype(F32)).astype(BF16)


def pack_kernel(
    block,
    mask_hbm,
    target_hbm,
    real_hbm,
    imag_hbm,
    pixel_hbm,
    owner_hbm,
    slot_hbm,
    weight_hbm,
    out_ref,
    rest_ref,
    taps_ref,
    mask_ref,
    target_ref,
    real_ref,
    imag_ref,
    pixel_ref,
    owner_ref,
    slot_ref,
    weight_ref,
    square,
    sems,
):
    rows, width = mask_hbm.shape
    half = rows // 2
    first = lax.axis_index("kern") * block
    left = pl.multiple_of(jnp.maximum(first - LANES, 0), LANES)
    right = pl.multiple_of(jnp.minimum(first + block, width - LANES), LANES)
    middle = pl.multiple_of(first, LANES)
    copies = []

    def fetch(source, place):
        copies.append(pltpu.make_async_copy(source, place, sems.at[len(copies)]))
        copies[-1].start()

    for source, place in ((mask_hbm, mask_ref), (target_hbm, target_ref)):
        fetch(source.at[:, pl.ds(middle, block)], place.at[:, LANES : LANES + block])
        fetch(source.at[:, pl.ds(left, LANES)], place.at[:, 0:LANES])
        fetch(source.at[:, pl.ds(right, LANES)], place.at[:, LANES + block :])
    fetch(real_hbm, real_ref)
    fetch(imag_hbm, imag_ref)
    fetch(pixel_hbm, pixel_ref)
    fetch(owner_hbm, owner_ref)
    fetch(slot_hbm, slot_ref)
    fetch(weight_hbm, weight_ref)
    square[...] = jnp.zeros_like(square)
    for copy in copies:
        copy.wait()

    whole = block + 2 * SIDE
    cut = slice(LANES - SIDE, LANES - SIDE + whole)
    column = first - SIDE + lax.broadcasted_iota(jnp.int32, (rows, whole), 1)
    inside = jnp.logical_and(column >= 0, column < width)
    mask = jnp.where(inside, mask_ref[...].astype(F32)[:, cut], 0.0)
    out_ref[0:rows, :] = mask.astype(BF16)
    target = target_ref[...].astype(F32)[:, cut].astype(BF16)
    out_ref[rows : rows + half, :] = target[:half]
    rest_ref[...] = target[half:]

    pixel = pixel_ref[...]
    pixel_high = pixel // LANES
    facts = [pixel_high, pixel - pixel_high * LANES, owner_ref[...], slot_ref[...]]
    facts = [fact.astype(F32) for fact in facts] + [part.astype(F32) for part in split3(weight_ref[...])]
    beside = whole // LANES
    layers = (out_ref.shape[0] - rows - half) // facts[0].shape[0]
    facts += [jnp.zeros_like(facts[0])] * (layers * beside - len(facts))
    lines = [jnp.concatenate(facts[at * beside : (at + 1) * beside], 1) for at in range(layers)]
    out_ref[rows + half :, :] = jnp.concatenate(lines, 0).astype(BF16)

    ksize = real_ref.shape[1]
    for kernel in range(real_ref.shape[0]):
        for part, ref in enumerate((real_ref, imag_ref)):
            square[0:ksize, 0:ksize] = ref[kernel].astype(F32)
            taps_ref[2 * kernel + part] = square[...].T[: taps_ref.shape[1]].astype(BF16)


def field_kernel(block, width, ksize, n_sets, weight_ref, *refs):
    sources = refs[: 3 + n_sets]
    here_ref, there_hbm, sums_ref = refs[3 + n_sets : 6 + n_sets]
    landed = refs[6 + n_sets : 9 + 2 * n_sets]
    own_ref, next_ref, rest_ref = landed[:3]
    tap_refs = landed[3:]
    (
        there_ref,
        taps32,
        mask_t,
        target_t,
        shifted,
        band,
        tail_band,
        fields,
        products,
        parts,
        row_hits,
        slot_hits,
        sems,
        out_sem,
    ) = refs[9 + 2 * n_sets :]
    radius = (ksize - 1) // 2
    per_set = tap_refs[0].shape[0]
    pairs = n_sets * per_set // 2
    rows = here_ref.shape[0]
    half = rows // 2
    window = 2 * rows
    span = block + 2 * radius
    tall = span + 2 * radius
    tall_out = block + GROUP
    groups = (ksize - 1) // GROUP
    height = 2 * pairs * rows
    kern_at = lax.axis_index("kern")
    last = lax.axis_index("tile") == lax.axis_size("tile") - 1

    copies = [
        pltpu.make_async_copy(source, place, sems.at[at])
        for at, (source, place) in enumerate(zip(sources, landed))
    ]
    for copy in copies:
        copy.start()
    for copy in copies[3:]:
        copy.wait()
    for index, ref in enumerate(tap_refs):
        taps32[index * per_set : (index + 1) * per_set] = ref[...].astype(F32)

    out_row = lax.broadcasted_iota(jnp.int32, (rows, window), 0) < half
    in_row = lax.broadcasted_iota(jnp.int32, (rows, window), 1) < rows
    keep = jnp.logical_or(out_row == in_row, jnp.logical_not(last))
    keep = keep.astype(F32)

    def toeplitz(component, b):
        row = jnp.broadcast_to(taps32[component, b : b + 1, :], (rows, window))
        return (pltpu.roll(row, 0, 1, stride=1, stride_axis=0) * keep).astype(BF16)

    def build(group):
        for j in range(GROUP):
            for component in range(2 * pairs):
                top = group * height + component * rows
                band[top : top + rows, j * window : (j + 1) * window] = toeplitz(
                    component, group * GROUP + j
                )

    for component in range(2 * pairs):
        tail_band[component * rows : (component + 1) * rows, :] = toeplitz(component, ksize - 1)
    build(0)

    for copy in copies[:3]:
        copy.wait()
    for piece in range(mask_t.shape[0] // LANES):
        lanes = slice(piece * LANES, (piece + 1) * LANES)
        both = jnp.concatenate([own_ref[0:rows, lanes], next_ref[0:rows, lanes]], 0)
        mask_t[lanes, :] = both.astype(F32).T
        one = jnp.concatenate([rest_ref[:, lanes], next_ref[rows : rows + half, lanes]], 0)
        target_t[lanes, :] = jnp.concatenate([one, one], 0).astype(F32).T
    base = SIDE - 2 * radius
    for j in range(GROUP):
        count = tall if j == 0 else tall - GROUP
        shifted[0:count, j * window : (j + 1) * window] = mask_t[base + j : base + j + count, :].astype(BF16)

    nt = (((1,), (1,)), ((), ()))
    fields[...] = lax.dot_general(
        shifted[2 * radius :, 0:window], tail_band[...], nt, preferred_element_type=F32
    )
    for group in range(groups):
        if group + 1 < groups:
            build(group + 1)
        fields[...] += lax.dot_general(
            shifted[group * GROUP : group * GROUP + span, :],
            band[group * height : (group + 1) * height, :],
            nt,
            preferred_element_type=F32,
        )

    weights = []
    for index in range(n_sets):
        source = lax.rem(kern_at - index + n_sets, n_sets)
        for kernel in range(per_set // 2):
            weights.append(weight_ref[source * (per_set // 2) + kernel])
    total_weight = weight_ref[0]
    for kernel in range(1, pairs):
        total_weight = total_weight + weight_ref[kernel]
    total_weight = jnp.full((1, window), total_weight, F32)
    intensity = jnp.zeros((span, window), F32)
    for kernel in range(pairs):
        field = fields[:, kernel * window : (kernel + 1) * window]
        intensity = intensity + weights[kernel] * field * field
    intensity = intensity + pltpu.roll(intensity, rows, 1)
    resist = jax.nn.sigmoid(steepness * (intensity / total_weight - threshold))
    target = target_t[SIDE - radius : SIDE - radius + span, :]
    slope = 2.0 * (resist - target) * steepness * resist * (1.0 - resist) / total_weight
    column = kern_at * block - radius + lax.broadcasted_iota(jnp.int32, (span, window), 0)
    slope = jnp.where(jnp.logical_and(column >= 0, column < width), slope, 0.0)
    for kernel in range(pairs):
        lanes = slice(kernel * window, (kernel + 1) * window)
        value = ((2.0 * weights[kernel]) * slope * fields[:, lanes]).astype(BF16)
        for group in range(groups):
            skip = (groups - 1 - group) * GROUP
            left = group * height + kernel * window
            products[:, left : left + window] = value[skip : skip + tall_out]

    beside = own_ref.shape[1] // LANES
    deep = 8

    def fact(index):
        top, left = index // beside * deep, index % beside * LANES
        lines = []
        for ref in (own_ref, next_ref):
            tile = ref[rows + half :, :].astype(F32)[top : top + deep, left : left + LANES]
            lines += [tile[at : at + 1] for at in range(deep)]
        return jnp.concatenate(lines, 1)

    pixel = (fact(0) * LANES + fact(1)).astype(jnp.int32)
    owner = fact(2).astype(jnp.int32)
    slot = fact(3).astype(jnp.int32)
    edge_weight = fact(4) + fact(5) + fact(6)
    edges = pixel.shape[1]
    row = pixel // block
    col = pixel - row * block
    row = row + jnp.where(lax.broadcasted_iota(jnp.int32, (1, edges), 1) < edges // 2, 0, rows)
    row_hit = (lax.broadcasted_iota(jnp.int32, (window, edges), 0) == row).astype(F32).astype(BF16)
    row_hits[0:window, :] = row_hit
    row_hits[window:, :] = row_hit
    slots = slot_hits.shape[0]
    slot_hits[...] = (lax.broadcasted_iota(jnp.int32, (slots, edges), 0) == slot).astype(F32).astype(BF16)

    for j in range(0, GROUP, 2):
        two = jnp.dot(products[...], band[:, j * window : (j + 2) * window], preferred_element_type=F32)
        parts[j] = two[:, :window]
        parts[j + 1] = two[:, window:]
    total = jnp.dot(products[0:block, (groups - 1) * height :], tail_band[...], preferred_element_type=F32)
    for j in range(GROUP):
        total = total + parts[j, GROUP - j : GROUP - j + block, :]
    for piece in range(block // LANES):
        lanes = slice(piece * LANES, (piece + 1) * LANES)
        turned = total[piece * LANES : (piece + 1) * LANES, :].T
        here_ref[:, lanes] = turned[:rows]
        there_ref[:, lanes] = turned[rows:]
    send = pltpu.make_async_copy(there_ref, there_hbm, out_sem)
    send.start()

    both = jnp.concatenate(split2(total), 1)
    picked = jnp.dot(both, row_hits[...], preferred_element_type=F32)
    col_hit = lax.broadcasted_iota(jnp.int32, (block, edges), 0) == col
    value = jnp.sum(jnp.where(col_hit, picked, 0.0), 0, keepdims=True) * edge_weight
    tiles = sums_ref.shape[0] // n_sets
    spread = jnp.where(lax.broadcasted_iota(jnp.int32, (tiles, edges), 0) == owner, value, 0.0)
    spread = jnp.concatenate([part.astype(F32) for part in split2(spread)], 0).astype(BF16)
    sums = lax.dot_general(spread, slot_hits[...], nt, preferred_element_type=F32)
    sums = sums[:tiles] + sums[tiles:]
    for tile in range(tiles):
        sums_ref[tile * n_sets : (tile + 1) * n_sets, :] = jnp.broadcast_to(
            sums[tile : tile + 1], (n_sets, slots)
        )
    send.wait()


def on_device(
    mask_field,
    target_map,
    kernel_real,
    kernel_imag,
    socs_weight,
    edge_pixel,
    edge_owner,
    edge_slot,
    edge_weight,
):
    rows, width = mask_field.shape
    half = rows // 2
    count, ksize = kernel_real.shape[:2]
    tiles, kerns = lax.axis_size("tile"), lax.axis_size("kern")
    block = width // kerns
    radius = (ksize - 1) // 2
    span = block + 2 * radius
    whole = block + 2 * SIDE
    groups = (ksize - 1) // GROUP
    edges = edge_pixel.shape[0]
    tap_rows = -(-ksize // 8) * 8
    layers = -(-FACTS // (whole // LANES))
    layers += layers % 2
    tall = rows + half + layers * 8
    tiled = (edges // LANES, LANES)
    own, rest, taps = pl.pallas_call(
        functools.partial(pack_kernel, block),
        out_shape=(
            jax.ShapeDtypeStruct((tall, whole), BF16),
            jax.ShapeDtypeStruct((half, whole), BF16),
            jax.ShapeDtypeStruct((2 * count, tap_rows, LANES), BF16),
        ),
        in_specs=[ANY] * 8,
        out_specs=(VMEM,) * 3,
        scratch_shapes=[
            pltpu.VMEM((rows, block + 2 * LANES), BF16),
            pltpu.VMEM((rows, block + 2 * LANES), jnp.int32),
            pltpu.VMEM(kernel_real.shape, BF16),
            pltpu.VMEM(kernel_imag.shape, BF16),
            pltpu.VMEM(tiled, jnp.int32),
            pltpu.VMEM(tiled, jnp.int32),
            pltpu.VMEM(tiled, jnp.int32),
            pltpu.VMEM(tiled, F32),
            pltpu.VMEM((LANES, LANES), F32),
            pltpu.SemaphoreType.DMA((12,)),
        ],
        name="pack",
    )(
        mask_field,
        target_map,
        kernel_real,
        kernel_imag,
        edge_pixel.reshape(tiled),
        edge_owner.reshape(tiled),
        edge_slot.reshape(tiled),
        edge_weight.reshape(tiled),
    )

    following = lax.ppermute(own, "tile", [(i, (i - 1) % tiles) for i in range(tiles)])
    tap_sets = [taps] + [
        lax.ppermute(taps, "kern", [(i, (i + step) % kerns) for i in range(kerns)])
        for step in range(1, kerns)
    ]
    sources = [own, following, rest, *tap_sets]
    components = 2 * count * kerns
    height = components * rows
    here, there, sums = pl.pallas_call(
        functools.partial(field_kernel, block, width, ksize, kerns),
        out_shape=(
            jax.ShapeDtypeStruct((rows, block), F32),
            jax.ShapeDtypeStruct((rows, block), F32),
            jax.ShapeDtypeStruct((tiles * kerns, POLY_DEV), F32),
        ),
        in_specs=[SMEM] + [ANY] * len(sources),
        out_specs=(VMEM, ANY, VMEM),
        scratch_shapes=[pltpu.VMEM(source.shape, source.dtype) for source in sources]
        + [
            pltpu.VMEM((rows, block), F32),
            pltpu.VMEM((components, tap_rows, LANES), F32),
            pltpu.VMEM((whole, LANES), F32),
            pltpu.VMEM((whole, LANES), F32),
            pltpu.VMEM((span + 2 * radius, GROUP * LANES), BF16),
            pltpu.VMEM((groups * height, GROUP * LANES), BF16),
            pltpu.VMEM((height, LANES), BF16),
            pltpu.VMEM((span, height), F32),
            pltpu.VMEM((block + GROUP, groups * height), BF16),
            pltpu.VMEM((GROUP, block + GROUP, LANES), F32),
            pltpu.VMEM((2 * LANES, 2 * edges), BF16),
            pltpu.VMEM((POLY_DEV, 2 * edges), BF16),
            pltpu.SemaphoreType.DMA((len(sources),)),
            pltpu.SemaphoreType.DMA,
        ],
        compiler_params=pltpu.CompilerParams(
            vmem_limit_bytes=groups * height * GROUP * LANES * 2 + (24 << 20)
        ),
        name="fields",
    )(socs_weight, *sources)
    came = lax.ppermute(there, "tile", [(i, (i + 1) % tiles) for i in range(tiles)])
    got = lax.all_to_all(sums, ("tile", "kern"), 0, 0, tiled=True)
    return (here + came, jnp.sum(got, 0))


def solution(mesh):
    placed = (
        P("tile", None),
        P("tile", None),
        P("kern", None, None),
        P("kern", None, None),
        P(),
        P(("tile", "kern")),
        P(("tile", "kern"), None),
        P(("tile", "kern")),
        P(("tile", "kern")),
    )
    return jax.shard_map(
        on_device,
        mesh=mesh,
        in_specs=placed,
        out_specs=(P("tile", "kern"), P("tile")),
        check_vma=False,
    )
```

```python
import functools

import jax
import jax.numpy as jnp
from jax import lax
from jax.experimental import pallas as pl
from jax.experimental.pallas import tpu as pltpu
from jax.sharding import PartitionSpec as P

POLY_DEV = 256

steepness = 8.0
threshold = 0.67

F32 = jnp.float32
BF16 = jnp.bfloat16
LANES = 128
SIDE = 64
GROUP = 16
FACTS = 7
HBM = pl.BlockSpec(memory_space=pltpu.HBM)
VMEM = pl.BlockSpec(memory_space=pltpu.VMEM)
SMEM = pl.BlockSpec(memory_space=pltpu.SMEM)


def split3(value):
    high = value.astype(BF16)
    rest = value - high.astype(F32)
    middle = rest.astype(BF16)
    low = (rest - middle.astype(F32)).astype(BF16)
    return high, middle, low


def split2(value):
    high = value.astype(BF16)
    return high, (value - high.astype(F32)).astype(BF16)


def pack_kernel(
    block,
    mask_hbm,
    target_hbm,
    real_hbm,
    imag_hbm,
    pixel_hbm,
    owner_hbm,
    slot_hbm,
    weight_hbm,
    out_ref,
    rest_ref,
    taps_ref,
    mask_ref,
    target_ref,
    real_ref,
    imag_ref,
    pixel_ref,
    owner_ref,
    slot_ref,
    weight_ref,
    square,
    sems,
):
    rows, width = mask_hbm.shape
    half = rows // 2
    first = lax.axis_index("kern") * block
    left = pl.multiple_of(jnp.maximum(first - LANES, 0), LANES)
    right = pl.multiple_of(jnp.minimum(first + block, width - LANES), LANES)
    middle = pl.multiple_of(first, LANES)
    copies = []

    def fetch(source, place):
        copies.append(pltpu.make_async_copy(source, place, sems.at[len(copies)]))
        copies[-1].start()

    for source, place in ((mask_hbm, mask_ref), (target_hbm, target_ref)):
        fetch(source.at[:, pl.ds(middle, block)], place.at[:, LANES : LANES + block])
        fetch(source.at[:, pl.ds(left, LANES)], place.at[:, 0:LANES])
        fetch(source.at[:, pl.ds(right, LANES)], place.at[:, LANES + block :])
    fetch(real_hbm, real_ref)
    fetch(imag_hbm, imag_ref)
    fetch(pixel_hbm, pixel_ref)
    fetch(owner_hbm, owner_ref)
    fetch(slot_hbm, slot_ref)
    fetch(weight_hbm, weight_ref)
    square[...] = jnp.zeros_like(square)
    for copy in copies:
        copy.wait()

    whole = block + 2 * SIDE
    cut = slice(LANES - SIDE, LANES - SIDE + whole)
    column = first - SIDE + lax.broadcasted_iota(jnp.int32, (rows, whole), 1)
    inside = jnp.logical_and(column >= 0, column < width)
    mask = jnp.where(inside, mask_ref[...].astype(F32)[:, cut], 0.0)
    out_ref[0:rows, :] = mask.astype(BF16)
    target = target_ref[...].astype(F32)[:, cut].astype(BF16)
    out_ref[rows : rows + half, :] = target[:half]
    rest_ref[...] = target[half:]

    pixel = pixel_ref[...]
    pixel_high = pixel // LANES
    facts = [pixel_high, pixel - pixel_high * LANES, owner_ref[...], slot_ref[...]]
    facts = [fact.astype(F32) for fact in facts] + [part.astype(F32) for part in split3(weight_ref[...])]
    beside = whole // LANES
    layers = (out_ref.shape[0] - rows - half) // facts[0].shape[0]
    facts += [jnp.zeros_like(facts[0])] * (layers * beside - len(facts))
    lines = [jnp.concatenate(facts[at * beside : (at + 1) * beside], 1) for at in range(layers)]
    out_ref[rows + half :, :] = jnp.concatenate(lines, 0).astype(BF16)

    ksize = real_ref.shape[1]
    for kernel in range(real_ref.shape[0]):
        for part, ref in enumerate((real_ref, imag_ref)):
            square[0:ksize, 0:ksize] = ref[kernel].astype(F32)
            taps_ref[2 * kernel + part] = square[...].T[: taps_ref.shape[1]].astype(BF16)


def field_kernel(block, width, ksize, n_sets, weight_ref, *refs):
    sources = refs[: 3 + n_sets]
    here_ref, there_hbm, sums_ref = refs[3 + n_sets : 6 + n_sets]
    landed = refs[6 + n_sets : 9 + 2 * n_sets]
    own_ref, next_ref, rest_ref = landed[:3]
    tap_refs = landed[3:]
    (
        there_ref,
        taps32,
        mask_t,
        target_t,
        shifted,
        band,
        tail_band,
        fields,
        products,
        parts,
        total_ref,
        spot_hits,
        slot_hits,
        sems,
        out_sem,
    ) = refs[9 + 2 * n_sets :]
    radius = (ksize - 1) // 2
    per_set = tap_refs[0].shape[0]
    pairs = n_sets * per_set // 2
    rows = here_ref.shape[0]
    half = rows // 2
    window = 2 * rows
    span = block + 2 * radius
    tall = span + 2 * radius
    tall_out = block + GROUP
    groups = (ksize - 1) // GROUP
    height = 2 * pairs * rows
    kern_at = lax.axis_index("kern")
    last = lax.axis_index("tile") == lax.axis_size("tile") - 1

    copies = [
        pltpu.make_async_copy(source, place, sems.at[at])
        for at, (source, place) in enumerate(zip(sources, landed))
    ]
    for copy in copies:
        copy.start()
    for copy in copies[3:]:
        copy.wait()
    for index, ref in enumerate(tap_refs):
        taps32[index * per_set : (index + 1) * per_set] = ref[...].astype(F32)

    out_row = lax.broadcasted_iota(jnp.int32, (rows, window), 0) < half
    in_row = lax.broadcasted_iota(jnp.int32, (rows, window), 1) < rows
    keep = jnp.logical_or(out_row == in_row, jnp.logical_not(last))
    keep = keep.astype(F32)

    def toeplitz(component, b):
        row = jnp.broadcast_to(taps32[component, b : b + 1, :], (rows, window))
        return (pltpu.roll(row, 0, 1, stride=1, stride_axis=0) * keep).astype(BF16)

    def build(group, side):
        for j in range(GROUP):
            for component in range(side * pairs, (side + 1) * pairs):
                top = group * height + component * rows
                band[top : top + rows, j * window : (j + 1) * window] = toeplitz(
                    component, group * GROUP + j
                )

    for component in range(2 * pairs):
        tail_band[component * rows : (component + 1) * rows, :] = toeplitz(component, ksize - 1)
    build(0, 0)

    for copy in copies[:3]:
        copy.wait()
    for piece in range(mask_t.shape[0] // LANES):
        lanes = slice(piece * LANES, (piece + 1) * LANES)
        both = jnp.concatenate([own_ref[0:rows, lanes], next_ref[0:rows, lanes]], 0)
        mask_t[lanes, :] = both.astype(F32).T
        one = jnp.concatenate([rest_ref[:, lanes], next_ref[rows : rows + half, lanes]], 0)
        target_t[lanes, :] = jnp.concatenate([one, one], 0).astype(F32).T
    base = SIDE - 2 * radius
    for j in range(GROUP):
        count = tall if j == 0 else tall - GROUP
        shifted[0:count, j * window : (j + 1) * window] = mask_t[base + j : base + j + count, :].astype(BF16)

    nt = (((1,), (1,)), ((), ()))
    fields[...] = lax.dot_general(
        shifted[2 * radius :, 0:window], tail_band[...], nt, preferred_element_type=F32
    )
    steps = [(group, side) for group in range(groups) for side in range(2)]
    part = height // 2
    for at, (group, side) in enumerate(steps):
        if at + 1 < len(steps):
            build(*steps[at + 1])
        fields[:, side * part : (side + 1) * part] += lax.dot_general(
            shifted[group * GROUP : group * GROUP + span, :],
            band[group * height + side * part : group * height + (side + 1) * part, :],
            nt,
            preferred_element_type=F32,
        )

    weights = []
    for index in range(n_sets):
        source = lax.rem(kern_at - index + n_sets, n_sets)
        for kernel in range(per_set // 2):
            weights.append(weight_ref[source * (per_set // 2) + kernel])
    total_weight = weight_ref[0]
    for kernel in range(1, pairs):
        total_weight = total_weight + weight_ref[kernel]
    total_weight = jnp.full((1, window), total_weight, F32)
    intensity = jnp.zeros((span, window), F32)
    for kernel in range(pairs):
        field = fields[:, kernel * window : (kernel + 1) * window]
        intensity = intensity + weights[kernel] * field * field
    intensity = intensity + pltpu.roll(intensity, rows, 1)
    resist = jax.nn.sigmoid(steepness * (intensity / total_weight - threshold))
    target = target_t[SIDE - radius : SIDE - radius + span, :]
    slope = 2.0 * (resist - target) * steepness * resist * (1.0 - resist) / total_weight
    column = kern_at * block - radius + lax.broadcasted_iota(jnp.int32, (span, window), 0)
    slope = jnp.where(jnp.logical_and(column >= 0, column < width), slope, 0.0)
    for kernel in range(pairs):
        lanes = slice(kernel * window, (kernel + 1) * window)
        value = ((2.0 * weights[kernel]) * slope * fields[:, lanes]).astype(BF16)
        for group in range(groups):
            skip = (groups - 1 - group) * GROUP
            left = group * height + kernel * window
            products[:, left : left + window] = value[skip : skip + tall_out]

    beside = own_ref.shape[1] // LANES
    deep = 8

    def fact(index):
        top, left = index // beside * deep, index % beside * LANES
        lines = []
        for ref in (own_ref, next_ref):
            tile = ref[rows + half :, :].astype(F32)[top : top + deep, left : left + LANES]
            lines += [tile[at : at + 1] for at in range(deep)]
        return jnp.concatenate(lines, 1)

    pixel = (fact(0) * LANES + fact(1)).astype(jnp.int32)
    owner = fact(2).astype(jnp.int32)
    slot = fact(3).astype(jnp.int32)
    edge_weight = fact(4) + fact(5) + fact(6)
    edges = pixel.shape[1]
    row = pixel // block
    col = pixel - row * block
    piece = col // LANES
    col = col - piece * LANES
    row = row + jnp.where(lax.broadcasted_iota(jnp.int32, (1, edges), 1) < edges // 2, 0, rows)
    pieces = block // LANES
    spot = piece * window + row
    spot_hits[...] = (
        (lax.broadcasted_iota(jnp.int32, (pieces * window, edges), 0) == spot).astype(F32).astype(BF16)
    )
    slots = slot_hits.shape[0]
    slot_hits[...] = (lax.broadcasted_iota(jnp.int32, (slots, edges), 0) == slot).astype(F32).astype(BF16)

    def moved(j):
        return parts[j, GROUP - j : GROUP - j + block, :]

    total_ref[...] = jnp.dot(
        products[0:block, (groups - 1) * height :], tail_band[...], preferred_element_type=F32
    )
    for j in range(0, GROUP, 2):
        two = jnp.dot(products[...], band[:, j * window : (j + 2) * window], preferred_element_type=F32)
        parts[j] = two[:, :window]
        parts[j + 1] = two[:, window:]
        if j >= 2:
            total_ref[...] += moved(j - 2) + moved(j - 1)
    total = total_ref[...] + moved(GROUP - 2) + moved(GROUP - 1)
    tiles_of_total = [total[piece * LANES : (piece + 1) * LANES, :] for piece in range(pieces)]
    for piece in range(pieces):
        lanes = slice(piece * LANES, (piece + 1) * LANES)
        turned = tiles_of_total[piece].T
        here_ref[:, lanes] = turned[:rows]
        there_ref[:, lanes] = turned[rows:]
    send = pltpu.make_async_copy(there_ref, there_hbm, out_sem)
    send.start()

    two = jnp.concatenate(split2(jnp.concatenate(tiles_of_total, 1)), 0)
    picked = jnp.dot(two, spot_hits[...], preferred_element_type=F32)
    picked = picked[:LANES] + picked[LANES:]
    col_hit = lax.broadcasted_iota(jnp.int32, (LANES, edges), 0) == col
    value = jnp.sum(jnp.where(col_hit, picked, 0.0), 0, keepdims=True) * edge_weight
    tiles = sums_ref.shape[0] // n_sets
    spread = jnp.where(lax.broadcasted_iota(jnp.int32, (tiles, edges), 0) == owner, value, 0.0)
    spread = jnp.concatenate([part.astype(F32) for part in split2(spread)], 0).astype(BF16)
    sums = lax.dot_general(spread, slot_hits[...], nt, preferred_element_type=F32)
    sums = sums[:tiles] + sums[tiles:]
    for tile in range(tiles):
        sums_ref[tile * n_sets : (tile + 1) * n_sets, :] = jnp.broadcast_to(
            sums[tile : tile + 1], (n_sets, slots)
        )
    send.wait()


def finish_kernel(here_hbm, came_hbm, got_hbm, grad_ref, sums_ref, here_ref, came_ref, got_ref, sems):
    copies = [
        pltpu.make_async_copy(source, place, sems.at[at])
        for at, (source, place) in enumerate(((here_hbm, here_ref), (came_hbm, came_ref), (got_hbm, got_ref)))
    ]
    for copy in copies:
        copy.start()
    for copy in copies:
        copy.wait()
    grad_ref[...] = here_ref[...] + came_ref[...]
    sums_ref[...] = jnp.sum(got_ref[...], 0, keepdims=True)


def on_device(
    mask_field,
    target_map,
    kernel_real,
    kernel_imag,
    socs_weight,
    edge_pixel,
    edge_owner,
    edge_slot,
    edge_weight,
):
    rows, width = mask_field.shape
    half = rows // 2
    count, ksize = kernel_real.shape[:2]
    tiles, kerns = lax.axis_size("tile"), lax.axis_size("kern")
    block = width // kerns
    radius = (ksize - 1) // 2
    span = block + 2 * radius
    whole = block + 2 * SIDE
    groups = (ksize - 1) // GROUP
    edges = edge_pixel.shape[0]
    tap_rows = -(-ksize // 8) * 8
    layers = -(-FACTS // (whole // LANES))
    layers += layers % 2
    tall = rows + half + layers * 8
    tiled = (edges // LANES, LANES)
    own, rest, taps = pl.pallas_call(
        functools.partial(pack_kernel, block),
        out_shape=(
            jax.ShapeDtypeStruct((tall, whole), BF16),
            jax.ShapeDtypeStruct((half, whole), BF16),
            jax.ShapeDtypeStruct((2 * count, tap_rows, LANES), BF16),
        ),
        in_specs=[HBM] * 8,
        out_specs=(VMEM,) * 3,
        scratch_shapes=[
            pltpu.VMEM((rows, block + 2 * LANES), BF16),
            pltpu.VMEM((rows, block + 2 * LANES), jnp.int32),
            pltpu.VMEM(kernel_real.shape, BF16),
            pltpu.VMEM(kernel_imag.shape, BF16),
            pltpu.VMEM(tiled, jnp.int32),
            pltpu.VMEM(tiled, jnp.int32),
            pltpu.VMEM(tiled, jnp.int32),
            pltpu.VMEM(tiled, F32),
            pltpu.VMEM((LANES, LANES), F32),
            pltpu.SemaphoreType.DMA((12,)),
        ],
        name="pack",
    )(
        mask_field,
        target_map,
        kernel_real,
        kernel_imag,
        edge_pixel.reshape(tiled),
        edge_owner.reshape(tiled),
        edge_slot.reshape(tiled),
        edge_weight.reshape(tiled),
    )

    following = lax.ppermute(own, "tile", [(i, (i - 1) % tiles) for i in range(tiles)])
    tap_sets = [taps] + [
        lax.ppermute(taps, "kern", [(i, (i + step) % kerns) for i in range(kerns)])
        for step in range(1, kerns)
    ]
    sources = [own, following, rest, *tap_sets]
    components = 2 * count * kerns
    height = components * rows
    here, there, sums = pl.pallas_call(
        functools.partial(field_kernel, block, width, ksize, kerns),
        out_shape=(
            jax.ShapeDtypeStruct((rows, block), F32),
            jax.ShapeDtypeStruct((rows, block), F32),
            jax.ShapeDtypeStruct((tiles * kerns, POLY_DEV), F32),
        ),
        in_specs=[SMEM] + [HBM] * len(sources),
        out_specs=(VMEM, HBM, VMEM),
        scratch_shapes=[pltpu.VMEM(source.shape, source.dtype) for source in sources]
        + [
            pltpu.VMEM((rows, block), F32),
            pltpu.VMEM((components, tap_rows, LANES), F32),
            pltpu.VMEM((whole, LANES), F32),
            pltpu.VMEM((whole, LANES), F32),
            pltpu.VMEM((span + 2 * radius, GROUP * LANES), BF16),
            pltpu.VMEM((groups * height, GROUP * LANES), BF16),
            pltpu.VMEM((height, LANES), BF16),
            pltpu.VMEM((span, height), F32),
            pltpu.VMEM((block + GROUP, groups * height), BF16),
            pltpu.VMEM((GROUP, block + GROUP, LANES), F32),
            pltpu.VMEM((block, LANES), F32),
            pltpu.VMEM((block, 2 * edges), BF16),
            pltpu.VMEM((POLY_DEV, 2 * edges), BF16),
            pltpu.SemaphoreType.DMA((len(sources),)),
            pltpu.SemaphoreType.DMA,
        ],
        compiler_params=pltpu.CompilerParams(
            vmem_limit_bytes=groups * height * GROUP * LANES * 2 + (24 << 20)
        ),
        name="fields",
    )(socs_weight, *sources)
    came = lax.ppermute(there, "tile", [(i, (i + 1) % tiles) for i in range(tiles)])
    got = lax.all_to_all(sums, ("tile", "kern"), 0, 0, tiled=True)
    mask_grad, sums = pl.pallas_call(
        finish_kernel,
        out_shape=(
            jax.ShapeDtypeStruct((rows, block), F32),
            jax.ShapeDtypeStruct((1, POLY_DEV), F32),
        ),
        in_specs=[HBM] * 3,
        out_specs=(VMEM,) * 2,
        scratch_shapes=[
            pltpu.VMEM((rows, block), F32),
            pltpu.VMEM((rows, block), F32),
            pltpu.VMEM(got.shape, F32),
            pltpu.SemaphoreType.DMA((3,)),
        ],
        name="finish",
    )(here, came, got)
    return (mask_grad, sums.reshape(-1))


def solution(mesh):
    placed = (
        P("tile", None),
        P("tile", None),
        P("kern", None, None),
        P("kern", None, None),
        P(),
        P(("tile", "kern")),
        P(("tile", "kern"), None),
        P(("tile", "kern")),
        P(("tile", "kern")),
    )
    return jax.shard_map(
        on_device,
        mesh=mesh,
        in_specs=placed,
        out_specs=(P("tile", "kern"), P("tile")),
        check_vma=False,
    )
```

```python
import functools

import jax
import jax.numpy as jnp
from jax import lax
from jax.experimental import pallas as pl
from jax.experimental.pallas import tpu as pltpu
from jax.sharding import PartitionSpec as P

POLY_DEV = 256

steepness = 8.0
threshold = 0.67

F32 = jnp.float32
BF16 = jnp.bfloat16
LANES = 128
SIDE = 64
GROUP = 16
FACTS = 7
HBM = pl.BlockSpec(memory_space=pltpu.HBM)
VMEM = pl.BlockSpec(memory_space=pltpu.VMEM)
SMEM = pl.BlockSpec(memory_space=pltpu.SMEM)


def split3(value):
    high = value.astype(BF16)
    rest = value - high.astype(F32)
    middle = rest.astype(BF16)
    low = (rest - middle.astype(F32)).astype(BF16)
    return high, middle, low


def split2(value):
    high = value.astype(BF16)
    return high, (value - high.astype(F32)).astype(BF16)


def pack_kernel(
    block,
    mask_hbm,
    target_hbm,
    real_hbm,
    imag_hbm,
    pixel_hbm,
    owner_hbm,
    slot_hbm,
    weight_hbm,
    out_ref,
    rest_ref,
    taps_ref,
    mask_ref,
    target_ref,
    real_ref,
    imag_ref,
    pixel_ref,
    owner_ref,
    slot_ref,
    weight_ref,
    square,
    sems,
):
    rows, width = mask_hbm.shape
    half = rows // 2
    first = lax.axis_index("kern") * block
    left = pl.multiple_of(jnp.maximum(first - LANES, 0), LANES)
    right = pl.multiple_of(jnp.minimum(first + block, width - LANES), LANES)
    middle = pl.multiple_of(first, LANES)
    copies = []

    def fetch(source, place):
        copies.append(pltpu.make_async_copy(source, place, sems.at[len(copies)]))
        copies[-1].start()

    for source, place in ((mask_hbm, mask_ref), (target_hbm, target_ref)):
        fetch(source.at[:, pl.ds(middle, block)], place.at[:, LANES : LANES + block])
        fetch(source.at[:, pl.ds(left, LANES)], place.at[:, 0:LANES])
        fetch(source.at[:, pl.ds(right, LANES)], place.at[:, LANES + block :])
    fetch(real_hbm, real_ref)
    fetch(imag_hbm, imag_ref)
    fetch(pixel_hbm, pixel_ref)
    fetch(owner_hbm, owner_ref)
    fetch(slot_hbm, slot_ref)
    fetch(weight_hbm, weight_ref)
    square[...] = jnp.zeros_like(square)
    for copy in copies:
        copy.wait()

    whole = block + 2 * SIDE
    cut = slice(LANES - SIDE, LANES - SIDE + whole)
    column = first - SIDE + lax.broadcasted_iota(jnp.int32, (rows, whole), 1)
    inside = jnp.logical_and(column >= 0, column < width)
    mask = jnp.where(inside, mask_ref[...].astype(F32)[:, cut], 0.0)
    out_ref[0:rows, :] = mask.astype(BF16)
    target = target_ref[...].astype(F32)[:, cut].astype(BF16)
    out_ref[rows : rows + half, :] = target[:half]
    rest_ref[...] = target[half:]

    pixel = pixel_ref[...]
    pixel_high = pixel // LANES
    facts = [pixel_high, pixel - pixel_high * LANES, owner_ref[...], slot_ref[...]]
    facts = [fact.astype(F32) for fact in facts] + [part.astype(F32) for part in split3(weight_ref[...])]
    beside = whole // LANES
    layers = (out_ref.shape[0] - rows - half) // facts[0].shape[0]
    facts += [jnp.zeros_like(facts[0])] * (layers * beside - len(facts))
    lines = [jnp.concatenate(facts[at * beside : (at + 1) * beside], 1) for at in range(layers)]
    out_ref[rows + half :, :] = jnp.concatenate(lines, 0).astype(BF16)

    ksize = real_ref.shape[1]
    for kernel in range(real_ref.shape[0]):
        for part, ref in enumerate((real_ref, imag_ref)):
            square[0:ksize, 0:ksize] = ref[kernel].astype(F32)
            taps_ref[2 * kernel + part] = square[...].T[: taps_ref.shape[1]].astype(BF16)


def field_kernel(block, width, ksize, n_sets, weight_ref, *refs):
    own_ref, next_ref, rest_ref = refs[:3]
    tap_refs = refs[3 : 3 + n_sets]
    here_ref, there_ref, sums_ref = refs[3 + n_sets : 6 + n_sets]
    (
        taps32,
        mask_t,
        target_t,
        shifted,
        band,
        tail_band,
        fields,
        products,
        parts,
        total_ref,
        spot_hits,
        slot_hits,
    ) = refs[6 + n_sets :]
    radius = (ksize - 1) // 2
    per_set = tap_refs[0].shape[0]
    pairs = n_sets * per_set // 2
    rows = here_ref.shape[0]
    half = rows // 2
    window = 2 * rows
    span = block + 2 * radius
    tall = span + 2 * radius
    tall_out = block + GROUP
    groups = (ksize - 1) // GROUP
    height = 2 * pairs * rows
    kern_at = lax.axis_index("kern")
    last = lax.axis_index("tile") == lax.axis_size("tile") - 1

    for index, ref in enumerate(tap_refs):
        taps32[index * per_set : (index + 1) * per_set] = ref[...].astype(F32)

    out_row = lax.broadcasted_iota(jnp.int32, (rows, window), 0) < half
    in_row = lax.broadcasted_iota(jnp.int32, (rows, window), 1) < rows
    keep = jnp.logical_or(out_row == in_row, jnp.logical_not(last))
    keep = keep.astype(F32)

    def toeplitz(component, b):
        row = jnp.broadcast_to(taps32[component, b : b + 1, :], (rows, window))
        return (pltpu.roll(row, 0, 1, stride=1, stride_axis=0) * keep).astype(BF16)

    def build(group, side):
        for j in range(GROUP):
            for component in range(side * pairs, (side + 1) * pairs):
                top = group * height + component * rows
                band[top : top + rows, j * window : (j + 1) * window] = toeplitz(
                    component, group * GROUP + j
                )

    for component in range(2 * pairs):
        tail_band[component * rows : (component + 1) * rows, :] = toeplitz(component, ksize - 1)
    build(0, 0)

    for piece in range(mask_t.shape[0] // LANES):
        lanes = slice(piece * LANES, (piece + 1) * LANES)
        both = jnp.concatenate([own_ref[0:rows, lanes], next_ref[0:rows, lanes]], 0)
        mask_t[lanes, :] = both.astype(F32).T
        one = jnp.concatenate([rest_ref[:, lanes], next_ref[rows : rows + half, lanes]], 0)
        target_t[lanes, :] = jnp.concatenate([one, one], 0).astype(F32).T
    base = SIDE - 2 * radius
    for j in range(GROUP):
        count = tall if j == 0 else tall - GROUP
        shifted[0:count, j * window : (j + 1) * window] = mask_t[base + j : base + j + count, :].astype(BF16)

    nt = (((1,), (1,)), ((), ()))
    fields[...] = lax.dot_general(
        shifted[2 * radius :, 0:window], tail_band[...], nt, preferred_element_type=F32
    )
    steps = [(group, side) for group in range(groups) for side in range(2)]
    part = height // 2
    for at, (group, side) in enumerate(steps):
        if at + 1 < len(steps):
            build(*steps[at + 1])
        fields[:, side * part : (side + 1) * part] += lax.dot_general(
            shifted[group * GROUP : group * GROUP + span, :],
            band[group * height + side * part : group * height + (side + 1) * part, :],
            nt,
            preferred_element_type=F32,
        )

    weights = []
    for index in range(n_sets):
        source = lax.rem(kern_at - index + n_sets, n_sets)
        for kernel in range(per_set // 2):
            weights.append(weight_ref[source * (per_set // 2) + kernel])
    total_weight = weight_ref[0]
    for kernel in range(1, pairs):
        total_weight = total_weight + weight_ref[kernel]
    total_weight = jnp.full((1, window), total_weight, F32)
    intensity = jnp.zeros((span, window), F32)
    for kernel in range(pairs):
        field = fields[:, kernel * window : (kernel + 1) * window]
        intensity = intensity + weights[kernel] * field * field
    intensity = intensity + pltpu.roll(intensity, rows, 1)
    resist = jax.nn.sigmoid(steepness * (intensity / total_weight - threshold))
    target = target_t[SIDE - radius : SIDE - radius + span, :]
    slope = 2.0 * (resist - target) * steepness * resist * (1.0 - resist) / total_weight
    column = kern_at * block - radius + lax.broadcasted_iota(jnp.int32, (span, window), 0)
    slope = jnp.where(jnp.logical_and(column >= 0, column < width), slope, 0.0)
    for kernel in range(pairs):
        lanes = slice(kernel * window, (kernel + 1) * window)
        value = ((2.0 * weights[kernel]) * slope * fields[:, lanes]).astype(BF16)
        for group in range(groups):
            skip = (groups - 1 - group) * GROUP
            left = group * height + kernel * window
            products[:, left : left + window] = value[skip : skip + tall_out]

    beside = own_ref.shape[1] // LANES
    deep = 8

    def fact(index):
        top, left = index // beside * deep, index % beside * LANES
        lines = []
        for ref in (own_ref, next_ref):
            tile = ref[rows + half :, :].astype(F32)[top : top + deep, left : left + LANES]
            lines += [tile[at : at + 1] for at in range(deep)]
        return jnp.concatenate(lines, 1)

    pixel = (fact(0) * LANES + fact(1)).astype(jnp.int32)
    owner = fact(2).astype(jnp.int32)
    slot = fact(3).astype(jnp.int32)
    edge_weight = fact(4) + fact(5) + fact(6)
    edges = pixel.shape[1]
    row = pixel // block
    col = pixel - row * block
    piece = col // LANES
    col = col - piece * LANES
    row = row + jnp.where(lax.broadcasted_iota(jnp.int32, (1, edges), 1) < edges // 2, 0, rows)
    pieces = block // LANES
    spot = piece * window + row
    spot_hits[...] = (
        (lax.broadcasted_iota(jnp.int32, (pieces * window, edges), 0) == spot).astype(F32).astype(BF16)
    )
    slots = slot_hits.shape[0]
    slot_hits[...] = (lax.broadcasted_iota(jnp.int32, (slots, edges), 0) == slot).astype(F32).astype(BF16)

    def moved(j):
        return parts[j, GROUP - j : GROUP - j + block, :]

    total_ref[...] = jnp.dot(
        products[0:block, (groups - 1) * height :], tail_band[...], preferred_element_type=F32
    )
    for j in range(0, GROUP, 2):
        two = jnp.dot(products[...], band[:, j * window : (j + 2) * window], preferred_element_type=F32)
        parts[j] = two[:, :window]
        parts[j + 1] = two[:, window:]
        if j >= 2:
            total_ref[...] += moved(j - 2) + moved(j - 1)
    total = total_ref[...] + moved(GROUP - 2) + moved(GROUP - 1)
    tiles_of_total = [total[piece * LANES : (piece + 1) * LANES, :] for piece in range(pieces)]
    for piece in range(pieces):
        lanes = slice(piece * LANES, (piece + 1) * LANES)
        turned = tiles_of_total[piece].T
        here_ref[:, lanes] = turned[:rows]
        there_ref[:, lanes] = turned[rows:]

    two = jnp.concatenate(split2(jnp.concatenate(tiles_of_total, 1)), 0)
    picked = jnp.dot(two, spot_hits[...], preferred_element_type=F32)
    picked = picked[:LANES] + picked[LANES:]
    col_hit = lax.broadcasted_iota(jnp.int32, (LANES, edges), 0) == col
    value = jnp.sum(jnp.where(col_hit, picked, 0.0), 0, keepdims=True) * edge_weight
    tiles = sums_ref.shape[0] // n_sets
    spread = jnp.where(lax.broadcasted_iota(jnp.int32, (tiles, edges), 0) == owner, value, 0.0)
    spread = jnp.concatenate([part.astype(F32) for part in split2(spread)], 0).astype(BF16)
    sums = lax.dot_general(spread, slot_hits[...], nt, preferred_element_type=F32)
    sums = sums[:tiles] + sums[tiles:]
    for tile in range(tiles):
        sums_ref[tile * n_sets : (tile + 1) * n_sets, :] = jnp.broadcast_to(
            sums[tile : tile + 1], (n_sets, slots)
        )


def finish_kernel(here_ref, came_ref, got_ref, grad_ref, sums_ref):
    grad_ref[...] = here_ref[...] + came_ref[...]
    sums_ref[...] = jnp.sum(got_ref[...], 0, keepdims=True)


def on_device(
    mask_field,
    target_map,
    kernel_real,
    kernel_imag,
    socs_weight,
    edge_pixel,
    edge_owner,
    edge_slot,
    edge_weight,
):
    rows, width = mask_field.shape
    half = rows // 2
    count, ksize = kernel_real.shape[:2]
    tiles, kerns = lax.axis_size("tile"), lax.axis_size("kern")
    block = width // kerns
    radius = (ksize - 1) // 2
    span = block + 2 * radius
    whole = block + 2 * SIDE
    groups = (ksize - 1) // GROUP
    edges = edge_pixel.shape[0]
    tap_rows = -(-ksize // 8) * 8
    layers = -(-FACTS // (whole // LANES))
    layers += layers % 2
    tall = rows + half + layers * 8
    tiled = (edges // LANES, LANES)
    own, rest, taps = pl.pallas_call(
        functools.partial(pack_kernel, block),
        out_shape=(
            jax.ShapeDtypeStruct((tall, whole), BF16),
            jax.ShapeDtypeStruct((half, whole), BF16),
            jax.ShapeDtypeStruct((2 * count, tap_rows, LANES), BF16),
        ),
        in_specs=[HBM] * 8,
        out_specs=(VMEM,) * 3,
        scratch_shapes=[
            pltpu.VMEM((rows, block + 2 * LANES), BF16),
            pltpu.VMEM((rows, block + 2 * LANES), jnp.int32),
            pltpu.VMEM(kernel_real.shape, BF16),
            pltpu.VMEM(kernel_imag.shape, BF16),
            pltpu.VMEM(tiled, jnp.int32),
            pltpu.VMEM(tiled, jnp.int32),
            pltpu.VMEM(tiled, jnp.int32),
            pltpu.VMEM(tiled, F32),
            pltpu.VMEM((LANES, LANES), F32),
            pltpu.SemaphoreType.DMA((12,)),
        ],
        compiler_params=pltpu.CompilerParams(vmem_limit_bytes=4 << 20),
        name="pack",
    )(
        *[
            pltpu.with_memory_space_constraint(array, pltpu.HBM)
            for array in (
                mask_field,
                target_map,
                kernel_real,
                kernel_imag,
                edge_pixel.reshape(tiled),
                edge_owner.reshape(tiled),
                edge_slot.reshape(tiled),
                edge_weight.reshape(tiled),
            )
        ]
    )

    following = lax.ppermute(own, "tile", [(i, (i - 1) % tiles) for i in range(tiles)])
    tap_sets = [taps] + [
        lax.ppermute(taps, "kern", [(i, (i + step) % kerns) for i in range(kerns)])
        for step in range(1, kerns)
    ]
    sources = [own, following, rest, *tap_sets]
    components = 2 * count * kerns
    height = components * rows
    here, there, sums = pl.pallas_call(
        functools.partial(field_kernel, block, width, ksize, kerns),
        out_shape=(
            jax.ShapeDtypeStruct((rows, block), F32),
            jax.ShapeDtypeStruct((rows, block), F32),
            jax.ShapeDtypeStruct((tiles * kerns, POLY_DEV), F32),
        ),
        in_specs=[SMEM] + [VMEM] * len(sources),
        out_specs=(VMEM,) * 3,
        scratch_shapes=[
            pltpu.VMEM((components, tap_rows, LANES), F32),
            pltpu.VMEM((whole, LANES), F32),
            pltpu.VMEM((whole, LANES), F32),
            pltpu.VMEM((span + 2 * radius, GROUP * LANES), BF16),
            pltpu.VMEM((groups * height, GROUP * LANES), BF16),
            pltpu.VMEM((height, LANES), BF16),
            pltpu.VMEM((span, height), F32),
            pltpu.VMEM((block + GROUP, groups * height), BF16),
            pltpu.VMEM((GROUP, block + GROUP, LANES), F32),
            pltpu.VMEM((block, LANES), F32),
            pltpu.VMEM((block, 2 * edges), BF16),
            pltpu.VMEM((POLY_DEV, 2 * edges), BF16),
        ],
        compiler_params=pltpu.CompilerParams(
            vmem_limit_bytes=groups * height * GROUP * LANES * 2 + (24 << 20)
        ),
        name="fields",
    )(socs_weight, *sources)
    came = lax.ppermute(there, "tile", [(i, (i + 1) % tiles) for i in range(tiles)])
    got = lax.all_to_all(sums, ("tile", "kern"), 0, 0, tiled=True)
    mask_grad, sums = pl.pallas_call(
        finish_kernel,
        out_shape=(
            jax.ShapeDtypeStruct((rows, block), F32),
            jax.ShapeDtypeStruct((1, POLY_DEV), F32),
        ),
        in_specs=[VMEM] * 3,
        out_specs=(VMEM,) * 2,
        compiler_params=pltpu.CompilerParams(vmem_limit_bytes=4 << 20),
        name="finish",
    )(here, came, got)
    return (mask_grad, sums.reshape(-1))


def solution(mesh):
    placed = (
        P("tile", None),
        P("tile", None),
        P("kern", None, None),
        P("kern", None, None),
        P(),
        P(("tile", "kern")),
        P(("tile", "kern"), None),
        P(("tile", "kern")),
        P(("tile", "kern")),
    )
    return jax.shard_map(
        on_device,
        mesh=mesh,
        in_specs=placed,
        out_specs=(P("tile", "kern"), P("tile")),
        check_vma=False,
    )
```

```python
import functools

import jax
import jax.numpy as jnp
from jax import lax
from jax.experimental import pallas as pl
from jax.experimental.pallas import tpu as pltpu
from jax.sharding import PartitionSpec as P

POLY_DEV = 256

steepness = 8.0
threshold = 0.67

F32 = jnp.float32
BF16 = jnp.bfloat16
LANES = 128
SIDE = 64
GROUP = 16
FACTS = 7
HBM = pl.BlockSpec(memory_space=pltpu.HBM)
VMEM = pl.BlockSpec(memory_space=pltpu.VMEM)


def split3(value):
    high = value.astype(BF16)
    rest = value - high.astype(F32)
    middle = rest.astype(BF16)
    low = (rest - middle.astype(F32)).astype(BF16)
    return high, middle, low


def split2(value):
    high = value.astype(BF16)
    return high, (value - high.astype(F32)).astype(BF16)


def pack_kernel(
    block,
    mask_hbm,
    target_hbm,
    real_hbm,
    imag_hbm,
    pixel_hbm,
    owner_hbm,
    slot_hbm,
    weight_hbm,
    socs_hbm,
    out_ref,
    rest_ref,
    taps_ref,
    socs_ref,
    mask_ref,
    target_ref,
    real_ref,
    imag_ref,
    pixel_ref,
    owner_ref,
    slot_ref,
    weight_ref,
    socs_smem,
    square,
    sems,
):
    rows, width = mask_hbm.shape
    half = rows // 2
    first = lax.axis_index("kern") * block
    left = pl.multiple_of(jnp.maximum(first - LANES, 0), LANES)
    right = pl.multiple_of(jnp.minimum(first + block, width - LANES), LANES)
    middle = pl.multiple_of(first, LANES)
    copies = []

    def fetch(source, place):
        copies.append(pltpu.make_async_copy(source, place, sems.at[len(copies)]))
        copies[-1].start()

    for source, place in ((mask_hbm, mask_ref), (target_hbm, target_ref)):
        fetch(source.at[:, pl.ds(middle, block)], place.at[:, LANES : LANES + block])
        fetch(source.at[:, pl.ds(left, LANES)], place.at[:, 0:LANES])
        fetch(source.at[:, pl.ds(right, LANES)], place.at[:, LANES + block :])
    fetch(real_hbm, real_ref)
    fetch(imag_hbm, imag_ref)
    fetch(pixel_hbm, pixel_ref)
    fetch(owner_hbm, owner_ref)
    fetch(slot_hbm, slot_ref)
    fetch(weight_hbm, weight_ref)
    fetch(socs_hbm, socs_smem)
    square[...] = jnp.zeros_like(square)
    for copy in copies:
        copy.wait()

    whole = block + 2 * SIDE
    cut = slice(LANES - SIDE, LANES - SIDE + whole)
    column = first - SIDE + lax.broadcasted_iota(jnp.int32, (rows, whole), 1)
    inside = jnp.logical_and(column >= 0, column < width)
    mask = jnp.where(inside, mask_ref[...].astype(F32)[:, cut], 0.0)
    out_ref[0:rows, :] = mask.astype(BF16)
    target = target_ref[...].astype(F32)[:, cut].astype(BF16)
    out_ref[rows : rows + half, :] = target[:half]
    rest_ref[...] = target[half:]

    pixel = pixel_ref[...]
    pixel_high = pixel // LANES
    facts = [pixel_high, pixel - pixel_high * LANES, owner_ref[...], slot_ref[...]]
    facts = [fact.astype(F32) for fact in facts] + [part.astype(F32) for part in split3(weight_ref[...])]
    beside = whole // LANES
    layers = (out_ref.shape[0] - rows - half) // facts[0].shape[0]
    facts += [jnp.zeros_like(facts[0])] * (layers * beside - len(facts))
    lines = [jnp.concatenate(facts[at * beside : (at + 1) * beside], 1) for at in range(layers)]
    out_ref[rows + half :, :] = jnp.concatenate(lines, 0).astype(BF16)

    count = real_ref.shape[0]
    kernels = socs_hbm.shape[0]
    total_weight = socs_smem[0]
    for kernel in range(1, kernels):
        total_weight = total_weight + socs_smem[kernel]
    for index in range(kernels // count):
        source = lax.bitwise_xor(lax.axis_index("kern"), jnp.int32(index)) * count
        for kernel in range(count):
            at = index * count + kernel
            socs_ref[at : at + 1, :] = jnp.full((1, LANES), socs_smem[source + kernel], F32)
    socs_ref[kernels : kernels + 1, :] = jnp.full((1, LANES), total_weight, F32)

    ksize = real_ref.shape[1]
    for kernel in range(real_ref.shape[0]):
        for part, ref in enumerate((real_ref, imag_ref)):
            square[0:ksize, 0:ksize] = ref[kernel].astype(F32)
            taps_ref[2 * kernel + part] = square[...].T[: taps_ref.shape[1]].astype(BF16)


def band_maker(ksize, tap_refs, taps32):
    per_set = tap_refs[0].shape[0]
    rows = LANES // 2
    window = 2 * rows
    last = lax.axis_index("tile") == lax.axis_size("tile") - 1
    for index, ref in enumerate(tap_refs):
        taps32[index * per_set : (index + 1) * per_set] = ref[...].astype(F32)

    out_row = lax.broadcasted_iota(jnp.int32, (rows, window), 0) < rows // 2
    in_row = lax.broadcasted_iota(jnp.int32, (rows, window), 1) < rows
    keep = jnp.logical_or(out_row == in_row, jnp.logical_not(last))
    keep = keep.astype(F32)

    def toeplitz(component, b):
        row = jnp.broadcast_to(taps32[component, b : b + 1, :], (rows, window))
        return (pltpu.roll(row, 0, 1, stride=1, stride_axis=0) * keep).astype(BF16)

    return toeplitz


def shift_mask(mask_t, shifted):
    tall = mask_t.shape[0]
    for j in range(GROUP):
        count = tall if j == 0 else tall - GROUP
        shifted[0:count, j * LANES : (j + 1) * LANES] = mask_t[j : j + count, :].astype(BF16)


def half_fields(ksize, toeplitz, base, offset, shifted, band, tail_band, fields):
    height = tail_band.shape[0]
    rows = LANES // 2
    components = height // rows
    window = 2 * rows
    radius = (ksize - 1) // 2
    span = fields.shape[0]
    groups = (ksize - 1) // GROUP
    part = GROUP // 2

    def build(group, side):
        for j in range(side * part, (side + 1) * part):
            for component in range(components):
                top = offset + group * height + component * rows
                band[top : top + rows, j * window : (j + 1) * window] = toeplitz(
                    base + component, group * GROUP + j
                )

    for component in range(components):
        tail_band[component * rows : (component + 1) * rows, :] = toeplitz(base + component, ksize - 1)
    build(0, 0)
    nt = (((1,), (1,)), ((), ()))
    fields[...] = lax.dot_general(
        shifted[2 * radius :, 0:window], tail_band[...], nt, preferred_element_type=F32
    )
    steps = [(group, side) for group in range(groups) for side in range(2)]
    for at, (group, side) in enumerate(steps):
        if at + 1 < len(steps):
            build(*steps[at + 1])
        lanes = slice(side * part * window, (side + 1) * part * window)
        top = offset + group * height
        fields[...] += lax.dot_general(
            shifted[group * GROUP : group * GROUP + span, lanes],
            band[top : top + height, lanes],
            nt,
            preferred_element_type=F32,
        )


def first_kernel(ksize, own_ref, next_ref, *refs):
    mask_t, fields, shifted, band, tail_band, taps32 = refs[-6:]
    tap_refs = refs[:-6]
    rows = LANES // 2
    for piece in range(mask_t.shape[0] // LANES):
        lanes = slice(piece * LANES, (piece + 1) * LANES)
        both = jnp.concatenate([own_ref[0:rows, lanes], next_ref[0:rows, lanes]], 0)
        mask_t[lanes, :] = both.astype(F32).T
    shift_mask(mask_t, shifted)
    toeplitz = band_maker(ksize, tap_refs, taps32)
    half_fields(ksize, toeplitz, 0, 0, shifted, band, tail_band, fields)


def second_kernel(block, width, ksize, n_sets, weight_ref, own_ref, next_ref, rest_ref, *refs):
    mask_t, fields_a = refs[:2]
    tap_refs = refs[2 : 2 + n_sets]
    here_ref, there_ref, sums_ref = refs[2 + n_sets : 5 + n_sets]
    (
        taps32,
        target_t,
        shifted,
        band,
        tail_a,
        tail_b,
        fields_b,
        products,
        parts,
        total_ref,
        spot_hits,
        slot_hits,
    ) = refs[5 + n_sets :]
    radius = (ksize - 1) // 2
    per_set = tap_refs[0].shape[0]
    pairs = n_sets * per_set // 2
    rows = here_ref.shape[0]
    half = rows // 2
    window = 2 * rows
    span = block + 2 * radius
    tall_out = block + GROUP
    groups = (ksize - 1) // GROUP
    height = tail_a.shape[0]
    deep_k = groups * height
    kern_at = lax.axis_index("kern")
    nt = (((1,), (1,)), ((), ()))

    shift_mask(mask_t, shifted)
    for piece in range(target_t.shape[0] // LANES):
        lanes = slice(piece * LANES, (piece + 1) * LANES)
        one = jnp.concatenate([rest_ref[:, lanes], next_ref[rows : rows + half, lanes]], 0)
        target_t[lanes, :] = jnp.concatenate([one, one], 0).astype(F32).T
    toeplitz = band_maker(ksize, tap_refs, taps32)
    half_fields(ksize, toeplitz, pairs, deep_k, shifted, band, tail_b, fields_b)

    def field(kernel):
        from_ref = (fields_a, fields_b)[kernel // (pairs // 2)]
        left = kernel % (pairs // 2) * window
        return from_ref[:, left : left + window]

    @pl.when(kern_at >= 0)
    def _():
        def rebuild(j):
            for group in range(groups):
                for component in range(pairs):
                    top = group * height + component * rows
                    band[top : top + rows, j * window : (j + 1) * window] = toeplitz(
                        component, group * GROUP + j
                    )

        for component in range(pairs):
            tail_a[component * rows : (component + 1) * rows, :] = toeplitz(component, ksize - 1)
        rebuild(0)
        rebuild(1)

        weights = [weight_ref[kernel : kernel + 1, :] for kernel in range(pairs)]
        total_weight = weight_ref[pairs : pairs + 1, :]
        intensity = jnp.zeros((span, window), F32)
        for kernel in range(pairs):
            intensity = intensity + weights[kernel] * field(kernel) * field(kernel)
        intensity = intensity + pltpu.roll(intensity, rows, 1)
        resist = jax.nn.sigmoid(steepness * (intensity / total_weight - threshold))
        target = target_t[SIDE - radius : SIDE - radius + span, :]
        slope = 2.0 * (resist - target) * steepness * resist * (1.0 - resist) / total_weight
        column = kern_at * block - radius + lax.broadcasted_iota(jnp.int32, (span, window), 0)
        slope = jnp.where(jnp.logical_and(column >= 0, column < width), slope, 0.0)
        for kernel in range(pairs):
            value = ((2.0 * weights[kernel]) * slope * field(kernel)).astype(BF16)
            for group in range(groups):
                skip = (groups - 1 - group) * GROUP
                left = (kernel // (pairs // 2) * groups + group) * height + kernel % (pairs // 2) * window
                products[:, left : left + window] = value[skip : skip + tall_out]

        beside = own_ref.shape[1] // LANES
        deep = 8

        def fact(index):
            top, left = index // beside * deep, index % beside * LANES
            lines = []
            for ref in (own_ref, next_ref):
                tile = ref[rows + half :, :].astype(F32)[top : top + deep, left : left + LANES]
                lines += [tile[at : at + 1] for at in range(deep)]
            return jnp.concatenate(lines, 1)

        pixel = (fact(0) * LANES + fact(1)).astype(jnp.int32)
        owner = fact(2).astype(jnp.int32)
        slot = fact(3).astype(jnp.int32)
        edge_weight = fact(4) + fact(5) + fact(6)
        edges = pixel.shape[1]
        row = pixel // block
        col = pixel - row * block
        piece = col // LANES
        col = col - piece * LANES
        row = row + jnp.where(lax.broadcasted_iota(jnp.int32, (1, edges), 1) < edges // 2, 0, rows)
        pieces = block // LANES
        spot = piece * window + row
        spot_hits[...] = (
            (lax.broadcasted_iota(jnp.int32, (pieces * window, edges), 0) == spot).astype(F32).astype(BF16)
        )
        slots = slot_hits.shape[0]
        slot_hits[...] = (lax.broadcasted_iota(jnp.int32, (slots, edges), 0) == slot).astype(F32).astype(BF16)

        def moved(j):
            return parts[j, GROUP - j : GROUP - j + block, :]

        total_ref[...] = jnp.dot(
            products[0:block, deep_k - height : deep_k], tail_a[...], preferred_element_type=F32
        ) + jnp.dot(products[0:block, 2 * deep_k - height :], tail_b[...], preferred_element_type=F32)
        for j in range(0, GROUP, 2):
            if j + 2 < GROUP:
                rebuild(j + 2)
                rebuild(j + 3)
            two = jnp.dot(products[...], band[:, j * window : (j + 2) * window], preferred_element_type=F32)
            parts[j] = two[:, :window]
            parts[j + 1] = two[:, window:]
            if j >= 2:
                total_ref[...] += moved(j - 2) + moved(j - 1)
        total = total_ref[...] + moved(GROUP - 2) + moved(GROUP - 1)
        tiles_of_total = [total[piece * LANES : (piece + 1) * LANES, :] for piece in range(pieces)]
        for piece in range(pieces):
            lanes = slice(piece * LANES, (piece + 1) * LANES)
            turned = tiles_of_total[piece].T
            here_ref[:, lanes] = turned[:rows]
            there_ref[:, lanes] = turned[rows:]

        two = jnp.concatenate(split2(jnp.concatenate(tiles_of_total, 1)), 0)
        picked = jnp.dot(two, spot_hits[...], preferred_element_type=F32)
        picked = picked[:LANES] + picked[LANES:]
        col_hit = lax.broadcasted_iota(jnp.int32, (LANES, edges), 0) == col
        value = jnp.sum(jnp.where(col_hit, picked, 0.0), 0, keepdims=True) * edge_weight
        tiles = sums_ref.shape[0] // n_sets
        spread = jnp.where(lax.broadcasted_iota(jnp.int32, (tiles, edges), 0) == owner, value, 0.0)
        spread = jnp.concatenate([part.astype(F32) for part in split2(spread)], 0).astype(BF16)
        sums = lax.dot_general(spread, slot_hits[...], nt, preferred_element_type=F32)
        sums = sums[:tiles] + sums[tiles:]
        for tile in range(tiles):
            sums_ref[tile * n_sets : (tile + 1) * n_sets, :] = jnp.broadcast_to(
                sums[tile : tile + 1], (n_sets, slots)
            )


def finish_kernel(here_ref, came_ref, got_ref, grad_ref, sums_ref):
    grad_ref[...] = here_ref[...] + came_ref[...]
    sums_ref[...] = jnp.sum(got_ref[...], 0, keepdims=True)


def on_device(
    mask_field,
    target_map,
    kernel_real,
    kernel_imag,
    socs_weight,
    edge_pixel,
    edge_owner,
    edge_slot,
    edge_weight,
):
    rows, width = mask_field.shape
    half = rows // 2
    count, ksize = kernel_real.shape[:2]
    tiles, kerns = lax.axis_size("tile"), lax.axis_size("kern")
    block = width // kerns
    radius = (ksize - 1) // 2
    span = block + 2 * radius
    whole = block + 2 * SIDE
    groups = (ksize - 1) // GROUP
    edges = edge_pixel.shape[0]
    tap_rows = -(-ksize // 8) * 8
    layers = -(-FACTS // (whole // LANES))
    layers += layers % 2
    message = rows + half + layers * 8
    tiled = (edges // LANES, LANES)
    own, rest, taps, weights = pl.pallas_call(
        functools.partial(pack_kernel, block),
        out_shape=(
            jax.ShapeDtypeStruct((message, whole), BF16),
            jax.ShapeDtypeStruct((half, whole), BF16),
            jax.ShapeDtypeStruct((2 * count, tap_rows, LANES), BF16),
            jax.ShapeDtypeStruct((-(-(count * kerns + 1) // 8) * 8, LANES), F32),
        ),
        in_specs=[HBM] * 9,
        out_specs=(VMEM,) * 4,
        scratch_shapes=[
            pltpu.VMEM((rows, block + 2 * LANES), BF16),
            pltpu.VMEM((rows, block + 2 * LANES), jnp.int32),
            pltpu.VMEM(kernel_real.shape, BF16),
            pltpu.VMEM(kernel_imag.shape, BF16),
            pltpu.VMEM(tiled, jnp.int32),
            pltpu.VMEM(tiled, jnp.int32),
            pltpu.VMEM(tiled, jnp.int32),
            pltpu.VMEM(tiled, F32),
            pltpu.SMEM(socs_weight.shape, F32),
            pltpu.VMEM((LANES, LANES), F32),
            pltpu.SemaphoreType.DMA((13,)),
        ],
        compiler_params=pltpu.CompilerParams(vmem_limit_bytes=4 << 20),
        name="pack",
    )(
        *[
            pltpu.with_memory_space_constraint(array, pltpu.HBM)
            for array in (
                mask_field,
                target_map,
                kernel_real,
                kernel_imag,
                edge_pixel.reshape(tiled),
                edge_owner.reshape(tiled),
                edge_slot.reshape(tiled),
                edge_weight.reshape(tiled),
                socs_weight,
            )
        ]
    )

    following = lax.ppermute(own, "tile", [(i, (i - 1) % tiles) for i in range(tiles)])
    tap_sets = [taps] + [
        lax.ppermute(taps, "kern", [(i, i ^ step) for i in range(kerns)])
        for step in range(1, kerns)
    ]
    components = 2 * count * kerns // 2
    height = components * rows
    tall = span + 2 * radius
    band_shape = (groups * height, GROUP * LANES)
    band_bytes = groups * height * GROUP * LANES * 2
    macs = span * ksize * LANES * height
    mask_t, fields = pl.pallas_call(
        functools.partial(first_kernel, ksize),
        out_shape=(
            jax.ShapeDtypeStruct((whole, LANES), F32),
            jax.ShapeDtypeStruct((span, height), F32),
        ),
        in_specs=[VMEM] * (2 + kerns // 2),
        out_specs=(VMEM,) * 2,
        scratch_shapes=[
            pltpu.VMEM((tall, GROUP * LANES), BF16),
            pltpu.VMEM(band_shape, BF16),
            pltpu.VMEM((height, LANES), BF16),
            pltpu.VMEM((components, tap_rows, LANES), F32),
        ],
        compiler_params=pltpu.CompilerParams(vmem_limit_bytes=band_bytes + (12 << 20)),
        cost_estimate=pl.CostEstimate(flops=2 * macs, bytes_accessed=4 * span * height, transcendentals=0),
        name="first",
    )(own, following, *tap_sets[: kerns // 2])
    here, there, sums = pl.pallas_call(
        functools.partial(second_kernel, block, width, ksize, kerns),
        out_shape=(
            jax.ShapeDtypeStruct((rows, block), F32),
            jax.ShapeDtypeStruct((rows, block), F32),
            jax.ShapeDtypeStruct((tiles * kerns, POLY_DEV), F32),
        ),
        in_specs=[VMEM] * (6 + kerns),
        out_specs=(VMEM,) * 3,
        scratch_shapes=[
            pltpu.VMEM((2 * components, tap_rows, LANES), F32),
            pltpu.VMEM((whole, LANES), F32),
            pltpu.VMEM((tall, GROUP * LANES), BF16),
            pltpu.VMEM((2 * band_shape[0], band_shape[1]), BF16),
            pltpu.VMEM((height, LANES), BF16),
            pltpu.VMEM((height, LANES), BF16),
            pltpu.VMEM((span, height), F32),
            pltpu.VMEM((block + GROUP, 2 * groups * height), BF16),
            pltpu.VMEM((GROUP, block + GROUP, LANES), F32),
            pltpu.VMEM((block, LANES), F32),
            pltpu.VMEM((block, 2 * edges), BF16),
            pltpu.VMEM((POLY_DEV, 2 * edges), BF16),
        ],
        compiler_params=pltpu.CompilerParams(vmem_limit_bytes=2 * band_bytes + (24 << 20)),
        cost_estimate=pl.CostEstimate(flops=6 * macs, bytes_accessed=4 * span * height, transcendentals=0),
        name="fields",
    )(weights, own, following, rest, mask_t, fields, *tap_sets)
    came = lax.ppermute(there, "tile", [(i, (i + 1) % tiles) for i in range(tiles)])
    got = lax.all_to_all(sums, ("tile", "kern"), 0, 0, tiled=True)
    mask_grad, sums = pl.pallas_call(
        finish_kernel,
        out_shape=(
            jax.ShapeDtypeStruct((rows, block), F32),
            jax.ShapeDtypeStruct((1, POLY_DEV), F32),
        ),
        in_specs=[VMEM] * 3,
        out_specs=(VMEM,) * 2,
        compiler_params=pltpu.CompilerParams(vmem_limit_bytes=4 << 20),
        name="finish",
    )(here, came, got)
    return (mask_grad, sums.reshape(-1))


def solution(mesh):
    placed = (
        P("tile", None),
        P("tile", None),
        P("kern", None, None),
        P("kern", None, None),
        P(),
        P(("tile", "kern")),
        P(("tile", "kern"), None),
        P(("tile", "kern")),
        P(("tile", "kern")),
    )
    return jax.shard_map(
        on_device,
        mesh=mesh,
        in_specs=placed,
        out_specs=(P("tile", "kern"), P("tile")),
        check_vma=False,
    )
```

```python
import functools

import jax
import jax.numpy as jnp
from jax import lax
from jax.experimental import pallas as pl
from jax.experimental.pallas import tpu as pltpu
from jax.sharding import PartitionSpec as P

POLY_DEV = 256

steepness = 8.0
threshold = 0.67

F32 = jnp.float32
BF16 = jnp.bfloat16
LANES = 128
SIDE = 64
GROUP = 16
FACTS = 7
HBM = pl.BlockSpec(memory_space=pltpu.HBM)
VMEM = pl.BlockSpec(memory_space=pltpu.VMEM)


def split3(value):
    high = value.astype(BF16)
    rest = value - high.astype(F32)
    middle = rest.astype(BF16)
    low = (rest - middle.astype(F32)).astype(BF16)
    return high, middle, low


def split2(value):
    high = value.astype(BF16)
    return high, (value - high.astype(F32)).astype(BF16)


def pack_kernel(
    block,
    mask_hbm,
    target_hbm,
    real_hbm,
    imag_hbm,
    pixel_hbm,
    owner_hbm,
    slot_hbm,
    weight_hbm,
    socs_hbm,
    out_ref,
    rest_ref,
    taps_ref,
    socs_ref,
    mask_ref,
    target_ref,
    real_ref,
    imag_ref,
    pixel_ref,
    owner_ref,
    slot_ref,
    weight_ref,
    socs_smem,
    square,
    sems,
):
    rows, width = mask_hbm.shape
    half = rows // 2
    first = lax.axis_index("kern") * block
    left = pl.multiple_of(jnp.maximum(first - LANES, 0), LANES)
    right = pl.multiple_of(jnp.minimum(first + block, width - LANES), LANES)
    middle = pl.multiple_of(first, LANES)
    copies = []

    def fetch(source, place):
        copies.append(pltpu.make_async_copy(source, place, sems.at[len(copies)]))
        copies[-1].start()

    for source, place in ((mask_hbm, mask_ref), (target_hbm, target_ref)):
        fetch(source.at[:, pl.ds(middle, block)], place.at[:, LANES : LANES + block])
        fetch(source.at[:, pl.ds(left, LANES)], place.at[:, 0:LANES])
        fetch(source.at[:, pl.ds(right, LANES)], place.at[:, LANES + block :])
    fetch(real_hbm, real_ref)
    fetch(imag_hbm, imag_ref)
    fetch(pixel_hbm, pixel_ref)
    fetch(owner_hbm, owner_ref)
    fetch(slot_hbm, slot_ref)
    fetch(weight_hbm, weight_ref)
    fetch(socs_hbm, socs_smem)
    square[...] = jnp.zeros_like(square)
    for copy in copies:
        copy.wait()

    whole = block + 2 * SIDE
    cut = slice(LANES - SIDE, LANES - SIDE + whole)
    column = first - SIDE + lax.broadcasted_iota(jnp.int32, (rows, whole), 1)
    inside = jnp.logical_and(column >= 0, column < width)
    mask = jnp.where(inside, mask_ref[...].astype(F32)[:, cut], 0.0)
    out_ref[0:rows, :] = mask.astype(BF16)
    target = target_ref[...].astype(F32)[:, cut].astype(BF16)
    out_ref[rows : rows + half, :] = target[:half]
    rest_ref[...] = target[half:]

    pixel = pixel_ref[...]
    pixel_high = pixel // LANES
    facts = [pixel_high, pixel - pixel_high * LANES, owner_ref[...], slot_ref[...]]
    facts = [fact.astype(F32) for fact in facts] + [part.astype(F32) for part in split3(weight_ref[...])]
    beside = whole // LANES
    layers = (out_ref.shape[0] - rows - half) // facts[0].shape[0]
    facts += [jnp.zeros_like(facts[0])] * (layers * beside - len(facts))
    lines = [jnp.concatenate(facts[at * beside : (at + 1) * beside], 1) for at in range(layers)]
    out_ref[rows + half :, :] = jnp.concatenate(lines, 0).astype(BF16)

    count = real_ref.shape[0]
    kernels = socs_hbm.shape[0]
    total_weight = socs_smem[0]
    for kernel in range(1, kernels):
        total_weight = total_weight + socs_smem[kernel]
    for index in range(kernels // count):
        source = lax.bitwise_xor(lax.axis_index("kern"), jnp.int32(index)) * count
        for kernel in range(count):
            at = index * count + kernel
            socs_ref[at : at + 1, :] = jnp.full((1, LANES), socs_smem[source + kernel], F32)
    socs_ref[kernels : kernels + 1, :] = jnp.full((1, LANES), total_weight, F32)

    ksize = real_ref.shape[1]
    for kernel in range(real_ref.shape[0]):
        for part, ref in enumerate((real_ref, imag_ref)):
            square[0:ksize, 0:ksize] = ref[kernel].astype(F32)
            taps_ref[2 * kernel + part] = square[...].T[: taps_ref.shape[1]].astype(BF16)


def band_maker(ksize, tap_refs, taps32):
    per_set = tap_refs[0].shape[0]
    rows = LANES // 2
    window = 2 * rows
    last = lax.axis_index("tile") == lax.axis_size("tile") - 1
    for index, ref in enumerate(tap_refs):
        taps32[index * per_set : (index + 1) * per_set] = ref[...].astype(F32)

    out_row = lax.broadcasted_iota(jnp.int32, (rows, window), 0) < rows // 2
    in_row = lax.broadcasted_iota(jnp.int32, (rows, window), 1) < rows
    keep = jnp.logical_or(out_row == in_row, jnp.logical_not(last))
    keep = keep.astype(F32)

    def toeplitz(component, b):
        row = jnp.broadcast_to(taps32[component, b : b + 1, :], (rows, window))
        return (pltpu.roll(row, 0, 1, stride=1, stride_axis=0) * keep).astype(BF16)

    return toeplitz


def shift_mask(mask_t, shifted):
    tall = mask_t.shape[0]
    for j in range(GROUP):
        count = tall if j == 0 else tall - GROUP
        shifted[0:count, j * LANES : (j + 1) * LANES] = mask_t[j : j + count, :].astype(BF16)


def half_fields(ksize, toeplitz, base, offset, shifted, band, tail_band, fields):
    height = tail_band.shape[0]
    rows = LANES // 2
    components = height // rows
    window = 2 * rows
    radius = (ksize - 1) // 2
    span = fields.shape[0]
    groups = (ksize - 1) // GROUP
    part = GROUP // 2

    def build(group, side):
        for j in range(side * part, (side + 1) * part):
            for component in range(components):
                top = offset + group * height + component * rows
                band[top : top + rows, j * window : (j + 1) * window] = toeplitz(
                    base + component, group * GROUP + j
                )

    for component in range(components):
        tail_band[component * rows : (component + 1) * rows, :] = toeplitz(base + component, ksize - 1)
    build(0, 0)
    nt = (((1,), (1,)), ((), ()))
    fields[...] = lax.dot_general(
        shifted[2 * radius :, 0:window], tail_band[...], nt, preferred_element_type=F32
    )
    steps = [(group, side) for group in range(groups) for side in range(2)]
    for at, (group, side) in enumerate(steps):
        if at + 1 < len(steps):
            build(*steps[at + 1])
        lanes = slice(side * part * window, (side + 1) * part * window)
        top = offset + group * height
        fields[...] += lax.dot_general(
            shifted[group * GROUP : group * GROUP + span, lanes],
            band[top : top + height, lanes],
            nt,
            preferred_element_type=F32,
        )


def first_kernel(ksize, own_ref, next_ref, *refs):
    mask_t, fields, shifted, band, tail_band, taps32 = refs[-6:]
    tap_refs = refs[:-6]
    rows = LANES // 2
    for piece in range(mask_t.shape[0] // LANES):
        lanes = slice(piece * LANES, (piece + 1) * LANES)
        both = jnp.concatenate([own_ref[0:rows, lanes], next_ref[0:rows, lanes]], 0)
        mask_t[lanes, :] = both.astype(F32).T
    shift_mask(mask_t, shifted)
    toeplitz = band_maker(ksize, tap_refs, taps32)
    half_fields(ksize, toeplitz, 0, 0, shifted, band, tail_band, fields)


def second_kernel(block, width, ksize, n_sets, weight_ref, own_ref, next_ref, rest_ref, *refs):
    mask_t, fields_a = refs[:2]
    tap_refs = refs[2 : 2 + n_sets]
    here_ref, there_ref, sums_ref = refs[2 + n_sets : 5 + n_sets]
    (
        taps32,
        target_t,
        shifted,
        band,
        tail_a,
        tail_b,
        fields_b,
        products,
        parts,
        total_ref,
        spot_hits,
        slot_hits,
    ) = refs[5 + n_sets :]
    radius = (ksize - 1) // 2
    per_set = tap_refs[0].shape[0]
    pairs = n_sets * per_set // 2
    rows = here_ref.shape[0]
    half = rows // 2
    window = 2 * rows
    span = block + 2 * radius
    tall_out = block + GROUP
    groups = (ksize - 1) // GROUP
    height = tail_a.shape[0]
    deep_k = groups * height
    kern_at = lax.axis_index("kern")
    nt = (((1,), (1,)), ((), ()))

    shift_mask(mask_t, shifted)
    toeplitz = band_maker(ksize, tap_refs, taps32)
    half_fields(ksize, toeplitz, pairs, deep_k, shifted, band, tail_b, fields_b)

    def field(kernel):
        from_ref = (fields_a, fields_b)[kernel // (pairs // 2)]
        left = kernel % (pairs // 2) * window
        return from_ref[:, left : left + window]

    @pl.when(kern_at >= 0)
    def _():
        def rebuild(j):
            for group in range(groups):
                for component in range(pairs):
                    top = group * height + component * rows
                    band[top : top + rows, j * window : (j + 1) * window] = toeplitz(
                        component, group * GROUP + j
                    )

        for component in range(pairs):
            tail_a[component * rows : (component + 1) * rows, :] = toeplitz(component, ksize - 1)
        rebuild(0)
        rebuild(1)

        for piece in range(target_t.shape[0] // LANES):
            lanes = slice(piece * LANES, (piece + 1) * LANES)
            one = jnp.concatenate([rest_ref[:, lanes], next_ref[rows : rows + half, lanes]], 0)
            target_t[lanes, :] = jnp.concatenate([one, one], 0).astype(F32).T
        weights = [weight_ref[kernel : kernel + 1, :] for kernel in range(pairs)]
        total_weight = weight_ref[pairs : pairs + 1, :]
        intensity = jnp.zeros((span, window), F32)
        for kernel in range(pairs):
            intensity = intensity + weights[kernel] * field(kernel) * field(kernel)
        intensity = intensity + pltpu.roll(intensity, rows, 1)
        resist = jax.nn.sigmoid(steepness * (intensity / total_weight - threshold))
        target = target_t[SIDE - radius : SIDE - radius + span, :]
        slope = 2.0 * (resist - target) * steepness * resist * (1.0 - resist) / total_weight
        column = kern_at * block - radius + lax.broadcasted_iota(jnp.int32, (span, window), 0)
        slope = jnp.where(jnp.logical_and(column >= 0, column < width), slope, 0.0)
        for kernel in range(pairs):
            value = ((2.0 * weights[kernel]) * slope * field(kernel)).astype(BF16)
            for group in range(groups):
                skip = (groups - 1 - group) * GROUP
                left = (kernel // (pairs // 2) * groups + group) * height + kernel % (pairs // 2) * window
                products[:, left : left + window] = value[skip : skip + tall_out]

        beside = own_ref.shape[1] // LANES
        deep = 8

        def fact(index):
            top, left = index // beside * deep, index % beside * LANES
            lines = []
            for ref in (own_ref, next_ref):
                tile = ref[rows + half :, :].astype(F32)[top : top + deep, left : left + LANES]
                lines += [tile[at : at + 1] for at in range(deep)]
            return jnp.concatenate(lines, 1)

        pixel = (fact(0) * LANES + fact(1)).astype(jnp.int32)
        owner = fact(2).astype(jnp.int32)
        slot = fact(3).astype(jnp.int32)
        edge_weight = fact(4) + fact(5) + fact(6)
        edges = pixel.shape[1]
        row = pixel // block
        col = pixel - row * block
        piece = col // LANES
        col = col - piece * LANES
        row = row + jnp.where(lax.broadcasted_iota(jnp.int32, (1, edges), 1) < edges // 2, 0, rows)
        pieces = block // LANES
        spot = piece * window + row
        slots = slot_hits.shape[0]

        def mark(hits, at, of, wanted):
            count = hits.shape[0] // of
            place = at * count + lax.broadcasted_iota(jnp.int32, (count, edges), 0)
            hits[at * count : (at + 1) * count, :] = (place == wanted).astype(F32).astype(BF16)


        def moved(j):
            return parts[j, GROUP - j : GROUP - j + block, :]

        total_ref[...] = jnp.dot(
            products[0:block, deep_k - height : deep_k], tail_a[...], preferred_element_type=F32
        ) + jnp.dot(products[0:block, 2 * deep_k - height :], tail_b[...], preferred_element_type=F32)
        for j in range(0, GROUP, 2):
            mark(spot_hits, j // 2, GROUP // 2, spot)
            mark(slot_hits, j // 2, GROUP // 2, slot)
            if j + 2 < GROUP:
                rebuild(j + 2)
                rebuild(j + 3)
            two = jnp.dot(products[...], band[:, j * window : (j + 2) * window], preferred_element_type=F32)
            parts[j] = two[:, :window]
            parts[j + 1] = two[:, window:]
            if j >= 2:
                total_ref[...] += moved(j - 2) + moved(j - 1)
        total = total_ref[...] + moved(GROUP - 2) + moved(GROUP - 1)
        tiles_of_total = [total[piece * LANES : (piece + 1) * LANES, :] for piece in range(pieces)]
        for piece in range(pieces):
            lanes = slice(piece * LANES, (piece + 1) * LANES)
            turned = tiles_of_total[piece].T
            here_ref[:, lanes] = turned[:rows]
            there_ref[:, lanes] = turned[rows:]

        @pl.when(kern_at >= 0)
        def _edges():
            two = jnp.concatenate(split2(jnp.concatenate(tiles_of_total, 1)), 0)
            picked = jnp.dot(two, spot_hits[...], preferred_element_type=F32)
            picked = picked[:LANES] + picked[LANES:]
            col_hit = lax.broadcasted_iota(jnp.int32, (LANES, edges), 0) == col
            value = jnp.sum(jnp.where(col_hit, picked, 0.0), 0, keepdims=True) * edge_weight
            tiles = sums_ref.shape[0] // n_sets
            spread = jnp.where(lax.broadcasted_iota(jnp.int32, (tiles, edges), 0) == owner, value, 0.0)
            spread = jnp.concatenate([part.astype(F32) for part in split2(spread)], 0).astype(BF16)
            sums = lax.dot_general(spread, slot_hits[...], nt, preferred_element_type=F32)
            sums = sums[:tiles] + sums[tiles:]
            for tile in range(tiles):
                sums_ref[tile * n_sets : (tile + 1) * n_sets, :] = jnp.broadcast_to(
                    sums[tile : tile + 1], (n_sets, slots)
                )


def finish_kernel(here_ref, came_ref, got_ref, grad_ref, sums_ref):
    grad_ref[...] = here_ref[...] + came_ref[...]
    sums_ref[...] = jnp.sum(got_ref[...], 0, keepdims=True)


def on_device(
    mask_field,
    target_map,
    kernel_real,
    kernel_imag,
    socs_weight,
    edge_pixel,
    edge_owner,
    edge_slot,
    edge_weight,
):
    rows, width = mask_field.shape
    half = rows // 2
    count, ksize = kernel_real.shape[:2]
    tiles, kerns = lax.axis_size("tile"), lax.axis_size("kern")
    block = width // kerns
    radius = (ksize - 1) // 2
    span = block + 2 * radius
    whole = block + 2 * SIDE
    groups = (ksize - 1) // GROUP
    edges = edge_pixel.shape[0]
    tap_rows = -(-ksize // 8) * 8
    layers = -(-FACTS // (whole // LANES))
    layers += layers % 2
    message = rows + half + layers * 8
    tiled = (edges // LANES, LANES)
    own, rest, taps, weights = pl.pallas_call(
        functools.partial(pack_kernel, block),
        out_shape=(
            jax.ShapeDtypeStruct((message, whole), BF16),
            jax.ShapeDtypeStruct((half, whole), BF16),
            jax.ShapeDtypeStruct((2 * count, tap_rows, LANES), BF16),
            jax.ShapeDtypeStruct((-(-(count * kerns + 1) // 8) * 8, LANES), F32),
        ),
        in_specs=[HBM] * 9,
        out_specs=(VMEM,) * 4,
        scratch_shapes=[
            pltpu.VMEM((rows, block + 2 * LANES), BF16),
            pltpu.VMEM((rows, block + 2 * LANES), jnp.int32),
            pltpu.VMEM(kernel_real.shape, BF16),
            pltpu.VMEM(kernel_imag.shape, BF16),
            pltpu.VMEM(tiled, jnp.int32),
            pltpu.VMEM(tiled, jnp.int32),
            pltpu.VMEM(tiled, jnp.int32),
            pltpu.VMEM(tiled, F32),
            pltpu.SMEM(socs_weight.shape, F32),
            pltpu.VMEM((LANES, LANES), F32),
            pltpu.SemaphoreType.DMA((13,)),
        ],
        compiler_params=pltpu.CompilerParams(vmem_limit_bytes=4 << 20),
        name="pack",
    )(
        *[
            pltpu.with_memory_space_constraint(array, pltpu.HBM)
            for array in (
                mask_field,
                target_map,
                kernel_real,
                kernel_imag,
                edge_pixel.reshape(tiled),
                edge_owner.reshape(tiled),
                edge_slot.reshape(tiled),
                edge_weight.reshape(tiled),
                socs_weight,
            )
        ]
    )

    following = lax.ppermute(own, "tile", [(i, (i - 1) % tiles) for i in range(tiles)])
    tap_sets = [taps] + [
        lax.ppermute(taps, "kern", [(i, i ^ step) for i in range(kerns)])
        for step in range(1, kerns)
    ]
    components = 2 * count * kerns // 2
    height = components * rows
    tall = span + 2 * radius
    band_shape = (groups * height, GROUP * LANES)
    band_bytes = groups * height * GROUP * LANES * 2
    macs = span * ksize * LANES * height
    mask_t, fields = pl.pallas_call(
        functools.partial(first_kernel, ksize),
        out_shape=(
            jax.ShapeDtypeStruct((whole, LANES), F32),
            jax.ShapeDtypeStruct((span, height), F32),
        ),
        in_specs=[VMEM] * (2 + kerns // 2),
        out_specs=(VMEM,) * 2,
        scratch_shapes=[
            pltpu.VMEM((tall, GROUP * LANES), BF16),
            pltpu.VMEM(band_shape, BF16),
            pltpu.VMEM((height, LANES), BF16),
            pltpu.VMEM((components, tap_rows, LANES), F32),
        ],
        compiler_params=pltpu.CompilerParams(vmem_limit_bytes=band_bytes + (12 << 20)),
        cost_estimate=pl.CostEstimate(flops=2 * macs, bytes_accessed=4 * span * height, transcendentals=0),
        name="first",
    )(own, following, *tap_sets[: kerns // 2])
    here, there, sums = pl.pallas_call(
        functools.partial(second_kernel, block, width, ksize, kerns),
        out_shape=(
            jax.ShapeDtypeStruct((rows, block), F32),
            jax.ShapeDtypeStruct((rows, block), F32),
            jax.ShapeDtypeStruct((tiles * kerns, POLY_DEV), F32),
        ),
        in_specs=[VMEM] * (6 + kerns),
        out_specs=(VMEM,) * 3,
        scratch_shapes=[
            pltpu.VMEM((2 * components, tap_rows, LANES), F32),
            pltpu.VMEM((whole, LANES), F32),
            pltpu.VMEM((tall, GROUP * LANES), BF16),
            pltpu.VMEM((2 * band_shape[0], band_shape[1]), BF16),
            pltpu.VMEM((height, LANES), BF16),
            pltpu.VMEM((height, LANES), BF16),
            pltpu.VMEM((span, height), F32),
            pltpu.VMEM((block + GROUP, 2 * groups * height), BF16),
            pltpu.VMEM((GROUP, block + GROUP, LANES), F32),
            pltpu.VMEM((block, LANES), F32),
            pltpu.VMEM((block, 2 * edges), BF16),
            pltpu.VMEM((POLY_DEV, 2 * edges), BF16),
        ],
        compiler_params=pltpu.CompilerParams(vmem_limit_bytes=2 * band_bytes + (24 << 20)),
        cost_estimate=pl.CostEstimate(flops=6 * macs, bytes_accessed=4 * span * height, transcendentals=0),
        name="fields",
    )(weights, own, following, rest, mask_t, fields, *tap_sets)
    came = lax.ppermute(there, "tile", [(i, (i + 1) % tiles) for i in range(tiles)])
    got = lax.all_to_all(sums, ("tile", "kern"), 0, 0, tiled=True)
    mask_grad, sums = pl.pallas_call(
        finish_kernel,
        out_shape=(
            jax.ShapeDtypeStruct((rows, block), F32),
            jax.ShapeDtypeStruct((1, POLY_DEV), F32),
        ),
        in_specs=[VMEM] * 3,
        out_specs=(VMEM,) * 2,
        compiler_params=pltpu.CompilerParams(vmem_limit_bytes=4 << 20),
        name="finish",
    )(here, came, got)
    return (mask_grad, sums.reshape(-1))


def solution(mesh):
    placed = (
        P("tile", None),
        P("tile", None),
        P("kern", None, None),
        P("kern", None, None),
        P(),
        P(("tile", "kern")),
        P(("tile", "kern"), None),
        P(("tile", "kern")),
        P(("tile", "kern")),
    )
    return jax.shard_map(
        on_device,
        mesh=mesh,
        in_specs=placed,
        out_specs=(P("tile", "kern"), P("tile")),
        check_vma=False,
    )
```
